256 devices in a mesh: seq: 32 (over y, x, core), tp: 8 (over z).
Axes of the slice: x: 4, y: 4, z: 8, core: 2. Of those that a mesh axis runs over, the one named last changes fastest.
Arguments:
- query: bfloat16 [32, 16384, 128], P('tp', 'seq'), may hold values from -12 to 12
- keyval: bfloat16 [2, 4, 16384, 128], P(None, None, 'seq'), may hold values from -6 to 6
- vert_blocks: int32 [32, 8], replicated, may hold values from 0 to 255, as said below
- slash_offsets: int32 [32, 8], replicated, may hold values from 0 to 255, as said below
- counts: int32 [32, 2], replicated, may hold values from 1 to 8, as said below
- out_weight: bfloat16 [4096, 8192], P('tp'), may hold values from -0.75 to 0.75
Outputs:
- projected: bfloat16 [16384, 8192], P(('seq', 'tp'))
The draws below stay inside these ranges and needn't reach their ends.
Inputs may be any that keep to these rules, and one draw needn't show every extreme that they name: `vert_blocks`: the 8 entries of each head's row are distinct; only the first counts[h, 0] are used. `slash_offsets`: the 8 entries of each head's row are distinct and the first is 0; only the first counts[h, 1] are used. `counts`: each column reaches 8 for some head.
All inputs are finite; a program needn't handle non-finite values.
Results may differ from the reference program's by a relative error of at most 0.017.
Values may be sent and summed in bfloat16 or wider, within the bound.
No kernel may reach another device: no remote copies, remote signals or barrier semaphores. Data moves between devices by JAX's collectives and lax.ppermute only.
A program may use at most 128 MiB of HBM per device.

```python
import math
import jax
import jax.numpy as jnp
from jax import lax

D = 8192
QUERY_HEAD_COUNT = 32
KEYVALUE_HEADS = 4
HEAD_WIDTH = 128
BLK = 64
SLOTS = 8
TOK_SEQ = 512
PROMPT_TOKENS = 16384
BLOCKS = 256
N_SEQ = 32
N_TP = 8


def draw_keyval(key, part):
    key = jax.random.fold_in(key, 3)
    simple_sample = jax.random.normal(key, (2, KEYVALUE_HEADS, PROMPT_TOKENS, HEAD_WIDTH), jnp.float32)
    return jnp.clip(simple_sample, -6.0, 6.0).astype(jnp.bfloat16)


def draw_query(key, part):
    key = jax.random.fold_in(key, 4)
    simple_sample = jax.random.normal(key, (QUERY_HEAD_COUNT, PROMPT_TOKENS, HEAD_WIDTH), jnp.float32)
    return jnp.clip(simple_sample, -6.0, 6.0).astype(jnp.bfloat16)


def draw_vert_blocks(key, part):
    key = jax.random.fold_in(key, 5)
    first_key, second_key = jax.random.split(key)
    head_keys = jax.random.split(first_key, QUERY_HEAD_COUNT)
    chosen_rows = jax.vmap(lambda one_key: jax.random.permutation(one_key, BLOCKS - 2)[:SLOTS] + 1)(head_keys)
    chosen_head = jax.random.randint(second_key, (2,), 0, QUERY_HEAD_COUNT)
    head_column = jnp.arange(QUERY_HEAD_COUNT, dtype=jnp.int32)[:, None]
    slot_row = jnp.arange(SLOTS, dtype=jnp.int32)[None, :]
    chosen_rows = jnp.where((head_column == chosen_head[0]) & (slot_row == 0), BLOCKS - 1, chosen_rows)
    chosen_rows = jnp.where((head_column == chosen_head[1]) & (slot_row == SLOTS - 1), 0, chosen_rows)
    return chosen_rows.astype(jnp.int32)


def draw_slash_offsets(key, part):
    key = jax.random.fold_in(key, 6)
    first_key, second_key = jax.random.split(key)
    head_keys = jax.random.split(first_key, QUERY_HEAD_COUNT)
    chosen_rows = jax.vmap(lambda one_key: jax.random.permutation(one_key, BLOCKS - 2)[:SLOTS - 1] + 1)(head_keys)
    chosen_rows = jnp.concatenate([jnp.zeros((QUERY_HEAD_COUNT, 1), jnp.int32), chosen_rows.astype(jnp.int32)], axis=1)
    chosen_head = jax.random.randint(second_key, (1,), 0, QUERY_HEAD_COUNT)
    head_column = jnp.arange(QUERY_HEAD_COUNT, dtype=jnp.int32)[:, None]
    slot_row = jnp.arange(SLOTS, dtype=jnp.int32)[None, :]
    chosen_rows = jnp.where((head_column == chosen_head[0]) & (slot_row == SLOTS - 1), BLOCKS - 1, chosen_rows)
    return chosen_rows.astype(jnp.int32)


def draw_counts(key, part):
    key = jax.random.fold_in(key, 7)
    first_key, second_key = jax.random.split(key)
    drawn_counts = jax.random.randint(first_key, (QUERY_HEAD_COUNT, 2), 1, SLOTS + 1)
    chosen_head = jax.random.randint(second_key, (1,), 0, QUERY_HEAD_COUNT)[0]
    head_column = jnp.arange(QUERY_HEAD_COUNT, dtype=jnp.int32)
    drawn_counts = drawn_counts.at[:, 0].set(jnp.where(head_column == chosen_head, SLOTS, drawn_counts[:, 0]))
    drawn_counts = drawn_counts.at[:, 1].set(jnp.where(head_column == (chosen_head + 1) % QUERY_HEAD_COUNT, SLOTS, drawn_counts[:, 1]))
    drawn_counts = drawn_counts.at[:, 0].set(jnp.where(head_column == (chosen_head + 2) % QUERY_HEAD_COUNT, 1, drawn_counts[:, 0]))
    return drawn_counts.astype(jnp.int32)


def level_of(stream_key, shape, shards, smallest, high):
    factor_of = 1.0
    for dim, blocks in shards:
        draws = jax.random.uniform(jax.random.fold_in(jax.random.fold_in(stream_key, 6), dim), (blocks,), jnp.float32, smallest / len(shards), high / len(shards))
        factor_of = factor_of * jnp.repeat(jnp.exp(draws), shape[dim] // blocks).reshape((-1,) + (1,) * (len(shape) - 1 - dim))
    return factor_of


def scatter_about(key, extent, deviation, most, cuts=(), kind=jnp.bfloat16):
    drawn = deviation * jax.random.normal(key, extent, jnp.float32)
    if cuts:
        drawn = drawn * level_of(key, extent, cuts, -0.22, 0.18)
    return jnp.clip(drawn, -most, most).astype(kind)


def setup_inputs(seed: int = 0) -> dict:
    splits = jax.random.split(jax.random.key(seed), 7)
    return {
        "query": draw_query(jax.random.fold_in(splits[6], 71), 0),
        "keyval": draw_keyval(jax.random.fold_in(splits[6], 71), 0),
        "vert_blocks": draw_vert_blocks(jax.random.fold_in(splits[6], 71), 0),
        "slash_offsets": draw_slash_offsets(jax.random.fold_in(splits[6], 71), 0),
        "counts": draw_counts(jax.random.fold_in(splits[6], 71), 0),
        "out_weight": scatter_about(splits[5], (QUERY_HEAD_COUNT * HEAD_WIDTH, D), (QUERY_HEAD_COUNT * HEAD_WIDTH // 64) ** -0.5, 0.75, ((0, 8),)),
    }


def plan_tiles(vertical, slash_list, list_counts, query_blocks):
    slot_count = vertical.shape[0]
    positions = jnp.arange(slot_count, dtype=jnp.int32)
    vert_live = positions < list_counts[0]
    vert_ok = vert_live[None, :] & (vertical[None, :] <= query_blocks[:, None])
    diag_block = query_blocks[:, None] - slash_list[None, :]
    covered = jnp.any((diag_block[:, :, None] == vertical[None, None, :]) & vert_live[None, None, :], axis=2)
    diag_ok = (positions < list_counts[1])[None, :] & (diag_block >= 0) & jnp.logical_not(covered)
    tile_index = jnp.concatenate([jnp.broadcast_to(vertical[None, :], diag_block.shape), jnp.maximum(diag_block, 0)], axis=1)
    tile_live = jnp.concatenate([vert_ok, diag_ok], axis=1)
    return (tile_index.astype(jnp.int32), tile_live)

def allowed_mask(tile_index, tile_live, query_blocks, block_size):
    offsets = jnp.arange(block_size, dtype=jnp.int32)
    query_pos = query_blocks[:, None] * block_size + offsets[None, :]
    key_pos = (tile_index[:, :, None] * block_size + offsets[None, None, :]).reshape(tile_index.shape[0], -1)
    live_keys = jnp.repeat(tile_live, block_size, axis=1)
    return live_keys[:, None, :] & (key_pos[:, None, :] <= query_pos[:, :, None])

def attend(queries, query_blocks, key_blocks, value_blocks, vertical, slash_list, list_counts):
    tile_index, tile_live = plan_tiles(vertical, slash_list, list_counts, query_blocks)
    group_count, block_size, head_size = queries.shape
    key_tile = key_blocks[tile_index].reshape(group_count, -1, head_size)
    value_tile = value_blocks[tile_index].reshape(group_count, -1, head_size)
    scores = jnp.einsum('gqd,gkd->gqk', queries.astype(jnp.float32), key_tile.astype(jnp.float32)) * (1.0 / math.sqrt(head_size))
    allowed = allowed_mask(tile_index, tile_live, query_blocks, block_size)
    masked = jnp.where(allowed, scores, -1e+30)
    row_top = lax.optimization_barrier(jnp.max(masked, axis=2, keepdims=True))
    weights = jnp.where(allowed, jnp.exp(masked - row_top), 0.0)
    row_total = lax.optimization_barrier(jnp.sum(weights, axis=2, keepdims=True))
    rounded = weights.astype(jnp.bfloat16)
    summed = jnp.einsum('gqk,gkd->gqd', rounded.astype(jnp.float32), value_tile.astype(jnp.float32))
    return (summed / row_total).astype(jnp.bfloat16)

def reference(query, keyval, vert_blocks, slash_offsets, counts, out_weight):
    group_width = QUERY_HEAD_COUNT // KEYVALUE_HEADS

    def one_head(head_index):
        kv_head = head_index // group_width
        key_blocks = lax.dynamic_index_in_dim(keyval[0], kv_head, 0, keepdims=False).reshape(BLOCKS, BLK, HEAD_WIDTH)
        value_blocks = lax.dynamic_index_in_dim(keyval[1], kv_head, 0, keepdims=False).reshape(BLOCKS, BLK, HEAD_WIDTH)
        query_rows = lax.dynamic_index_in_dim(query, head_index, 0, keepdims=False).reshape(BLOCKS // 8, 8, BLK, HEAD_WIDTH)
        vertical = lax.dynamic_index_in_dim(vert_blocks, head_index, 0, keepdims=False)
        slash_list = lax.dynamic_index_in_dim(slash_offsets, head_index, 0, keepdims=False)
        list_counts = lax.dynamic_index_in_dim(counts, head_index, 0, keepdims=False)
        starts = jnp.arange(BLOCKS // 8, dtype=jnp.int32) * 8

        def one_group(group_pair):
            queries, first_block = group_pair
            query_blocks = (first_block + jnp.arange(8, dtype=jnp.int32)).astype(jnp.int32)
            return attend(queries, query_blocks, key_blocks, value_blocks, vertical, slash_list, list_counts)
        return lax.map(one_group, (query_rows, starts)).reshape(PROMPT_TOKENS, HEAD_WIDTH)
    attended = lax.map(one_head, jnp.arange(QUERY_HEAD_COUNT, dtype=jnp.int32))
    weight_full = out_weight.astype(jnp.float32).reshape(QUERY_HEAD_COUNT, HEAD_WIDTH, D)
    per_group = QUERY_HEAD_COUNT // N_TP

    def one_slab(first_row):
        rows = lax.dynamic_slice_in_dim(attended, first_row, TOK_SEQ, 1).astype(jnp.float32)
        summed = jnp.zeros((TOK_SEQ, D), jnp.float32)
        for tp_slot in range(N_TP):
            first_head = tp_slot * per_group
            part_sum = lax.dot_general(rows[first_head:first_head + per_group], weight_full[first_head:first_head + per_group], (((0, 2), (0, 1)), ((), ())))
            part_sum = lax.optimization_barrier(part_sum.astype(jnp.bfloat16))
            summed = summed + part_sum.astype(jnp.float32)
        return summed.astype(jnp.bfloat16)
    slabs = lax.map(one_slab, jnp.arange(N_SEQ, dtype=jnp.int32) * TOK_SEQ)
    return slabs.reshape(PROMPT_TOKENS, D)
```

```python
import functools
import math

import jax
import jax.numpy as jnp
from jax import lax
from jax.experimental import pallas as pl
from jax.experimental.pallas import tpu as pltpu
from jax.sharding import PartitionSpec as P

BLK = 64
NY, NX, NC = 4, 4, 2
DEAD = 1 << 20
SCALE = math.log2(math.e)


def seq_perm(move):
    pairs = []
    for y in range(NY):
        for x in range(NX):
            for c in range(NC):
                ty, tx, tc = move(y, x, c)
                pairs.append(((y * NX + x) * NC + c, ((ty % NY) * NX + tx % NX) * NC + tc))
    return pairs


A_UP = seq_perm(lambda y, x, c: (y, x + 1, c) if c == 0 else (y + 1, x, c))
A_DOWN = seq_perm(lambda y, x, c: (y, x - 1, c) if c == 0 else (y - 1, x, c))
B_UP = seq_perm(lambda y, x, c: (y + 1, x, c) if c == 0 else (y, x + 1, c))
B_DOWN = seq_perm(lambda y, x, c: (y - 1, x, c) if c == 0 else (y, x - 1, c))
SWAP = seq_perm(lambda y, x, c: (y, x, 1 - c))


def send(a, pairs):
    return lax.ppermute(a, "seq", pairs)


def gather_keyval(own):
    up, down = send(own, A_UP), send(own, A_DOWN)
    far = jnp.stack([send(up[0], A_UP), send(down[1], A_DOWN)])
    line = jnp.stack([own, up, down, far])
    up2, down2 = send(line, B_UP), send(line, B_DOWN)
    far_k, far_v = send(up2[:, 0], B_UP), send(down2[:, 1], B_DOWN)
    mine = [line, up2, down2, far_k, far_v]
    return mine + [send(a, SWAP) for a in mine]


def shard_slots(seq_index):
    shard = jnp.arange(NY * NX * NC, dtype=jnp.int32)

    def parts(i):
        return i // (NX * NC), (i // NC) % NX, i % NC

    ys, xs, cs = parts(shard)
    y0, x0, c0 = parts(seq_index)
    order = jnp.array([0, 2, 3, 1], jnp.int32)
    in_y, in_x = order[(ys - y0) % NY], order[(xs - x0) % NX]
    first = jnp.where(cs == 0, in_x, in_y)
    second = jnp.where(cs == 0, in_y, in_x)
    return (cs != c0) * 16 + second * 4 + first


def attend_kernel(
    slots_ref, vert_ref, diag_ref, q_ref, kpv_ref, kpd_ref,
    l0, u0, d0, fk0, fv0, l1, u1, d1, fk1, fv1,
    o_ref, kbuf, vbuf, sv_ref, pv_ref, od_ref, tot_ref, sems,
):
    heads, rows, width = q_ref.shape
    blocks = rows // BLK
    per = rows // BLK
    copies = ([], [])
    for side, (line, up, down, fk, fv) in enumerate(((l0, u0, d0, fk0, fv0), (l1, u1, d1, fk1, fv1))):
        for which, buf in enumerate((kbuf, vbuf)):
            for j, src in enumerate((line, up, down, (fk, fv)[which])):
                for i in range(4):
                    piece = src.at[i] if j == 3 else src.at[i, which]
                    slot = side * 16 + j * 4 + i
                    copies[which].append(
                        pltpu.make_async_copy(piece, buf.at[slot], sems.at[which, slot])
                    )
    for c in copies[0] + copies[1]:
        c.start()
    for c in copies[0]:
        c.wait()
    for c in copies[1]:
        c.wait()

    def tile(buf, block):
        return buf[slots_ref[block // per], pl.ds(pl.multiple_of((block % per) * BLK, BLK), BLK), :]

    scale = SCALE / math.sqrt(width)
    nt = (((1,), (1,)), ((), ()))

    def one_head(h, carry):
        verts = [vert_ref[h, c] for c in range(8)]
        k_v = jnp.concatenate([tile(kbuf, v) for v in verts], axis=0)
        sv_ref[...] = lax.dot_general(q_ref[h], k_v, nt, preferred_element_type=jnp.float32)
        kpv = kpv_ref[h]
        for b in range(blocks):
            r = slice(b * BLK, (b + 1) * BLK)
            diags = [diag_ref[h * blocks + b, c] for c in range(8)]
            k_d = jnp.concatenate([tile(kbuf, v) for v in diags], axis=0)
            s_d = lax.dot_general(q_ref[h, r, :], k_d, nt, preferred_element_type=jnp.float32)
            s_v = sv_ref[r, :]
            qpos = b * BLK + lax.broadcasted_iota(jnp.int32, (BLK, 1), 0)
            s_d = jnp.where(kpd_ref[h * blocks + b] <= qpos, s_d, -1e30)
            s_v = jnp.where(kpv <= qpos, s_v, -1e30)
            top = jnp.maximum(
                jnp.max(s_d, axis=1, keepdims=True), jnp.max(s_v, axis=1, keepdims=True)
            )
            p_d = jnp.exp2((s_d - top) * scale)
            p_v = jnp.exp2((s_v - top) * scale)
            tot_ref[r, :] = jnp.sum(p_d, axis=1, keepdims=True) + jnp.sum(
                p_v, axis=1, keepdims=True
            )
            pv_ref[r, :] = p_v.astype(jnp.bfloat16)
            v_d = jnp.concatenate([tile(vbuf, v) for v in diags], axis=0)
            od_ref[r, :] = jnp.dot(
                p_d.astype(jnp.bfloat16), v_d, preferred_element_type=jnp.float32
            )
        v_v = jnp.concatenate([tile(vbuf, v) for v in verts], axis=0)
        o_v = jnp.dot(pv_ref[...], v_v, preferred_element_type=jnp.float32)
        o_ref[h] = ((o_v + od_ref[...]) / tot_ref[...]).astype(jnp.bfloat16)
        return carry

    lax.fori_loop(0, heads, one_head, 0)


def attend(query, pieces, slots, vertical, slash, counts, seq_index):
    heads, rows, width = query.shape
    blocks = rows // BLK
    slot = jnp.arange(8, dtype=jnp.int32)
    first = seq_index * blocks
    vert_live = slot[None, :] < counts[:, 0:1]
    diag = first + jnp.arange(blocks, dtype=jnp.int32)[None, :, None] - slash[:, None, :]
    covered = jnp.any(
        (diag[:, :, :, None] == vertical[:, None, None, :]) & vert_live[:, None, None, :], axis=3
    )
    diag_live = (slot < counts[:, 1:2])[:, None, :] & (diag >= 0) & jnp.logical_not(covered)
    within = jnp.arange(BLK, dtype=jnp.int32)
    kpv = jnp.where(
        vert_live[:, :, None], (vertical - first)[:, :, None] * BLK + within, DEAD
    ).reshape(heads, 1, 8 * BLK)
    kpd = jnp.where(
        diag_live[:, :, :, None], (diag - first)[:, :, :, None] * BLK + within, DEAD
    ).reshape(heads * blocks, 1, 8 * BLK)
    diag = jnp.maximum(diag, 0).reshape(heads * blocks, 8)
    smem = pl.BlockSpec(memory_space=pltpu.SMEM)
    vmem = pl.BlockSpec(memory_space=pltpu.VMEM)
    hbm = pl.BlockSpec(memory_space=pl.ANY)
    f32 = jnp.float32
    return pl.pallas_call(
        attend_kernel,
        out_shape=jax.ShapeDtypeStruct((heads, rows, width), jnp.bfloat16),
        in_specs=[smem] * 3 + [vmem] * 3 + [hbm] * len(pieces),
        out_specs=vmem,
        scratch_shapes=[
            pltpu.VMEM((32, rows, width), jnp.bfloat16),
            pltpu.VMEM((32, rows, width), jnp.bfloat16),
            pltpu.VMEM((rows, 8 * BLK), f32),
            pltpu.VMEM((rows, 8 * BLK), jnp.bfloat16),
            pltpu.VMEM((rows, width), f32),
            pltpu.VMEM((rows, 1), f32),
            pltpu.SemaphoreType.DMA((2, 32)),
        ],
        compiler_params=pltpu.CompilerParams(vmem_limit_bytes=24 * 2**20),
        name="attend",
    )(slots, vertical, diag, query, kpv, kpd, *pieces)


def per_device(query, keyval, vert_blocks, slash_offsets, counts, out_weight):
    heads, rows, width = query.shape
    seq_index = lax.axis_index("seq")
    tp_index = lax.axis_index("tp")
    kv_head = tp_index // (lax.axis_size("tp") // keyval.shape[1])
    own = lax.dynamic_index_in_dim(keyval, kv_head, 1, keepdims=False)
    pieces = gather_keyval(own)

    def mine(a):
        return lax.dynamic_slice_in_dim(a, tp_index * heads, heads, 0)

    attended = attend(
        query, pieces, shard_slots(seq_index), mine(vert_blocks), mine(slash_offsets),
        mine(counts), seq_index,
    )
    weight_heads = out_weight.reshape(heads, width, -1)
    partial = lax.dot_general(
        attended, weight_heads, (((0, 2), (0, 1)), ((), ())), preferred_element_type=jnp.float32
    ).astype(jnp.bfloat16)
    return lax.psum_scatter(partial, "tp", scatter_dimension=0, tiled=True)


def solution(mesh):
    return jax.shard_map(
        per_device,
        mesh=mesh,
        in_specs=(P("tp", "seq", None), P(None, None, "seq", None), P(), P(), P(), P("tp", None)),
        out_specs=P(("seq", "tp"), None),
        check_vma=False,
    )
```

```python
import functools
import math

import jax
import jax.numpy as jnp
from jax import lax
from jax.experimental import pallas as pl
from jax.experimental.pallas import tpu as pltpu
from jax.sharding import PartitionSpec as P

BLK = 64
NY, NX, NC = 4, 4, 2
DEAD = 1 << 20
SCALE = math.log2(math.e)


def seq_perm(move):
    pairs = []
    for y in range(NY):
        for x in range(NX):
            for c in range(NC):
                ty, tx, tc = move(y, x, c)
                pairs.append(((y * NX + x) * NC + c, ((ty % NY) * NX + tx % NX) * NC + tc))
    return pairs


A_UP = seq_perm(lambda y, x, c: (y, x + 1, c) if c == 0 else (y + 1, x, c))
A_DOWN = seq_perm(lambda y, x, c: (y, x - 1, c) if c == 0 else (y - 1, x, c))
B_UP = seq_perm(lambda y, x, c: (y + 1, x, c) if c == 0 else (y, x + 1, c))
B_DOWN = seq_perm(lambda y, x, c: (y - 1, x, c) if c == 0 else (y, x - 1, c))
def pair(v, c):
    return (v ^ 1) if c == 0 else (v + 1 if v % 2 else v - 1)


PAIR_X = seq_perm(lambda y, x, c: (y, pair(x, c), c))
PAIR_Y = seq_perm(lambda y, x, c: (pair(y, c), x, c))
PAIR_XY = seq_perm(lambda y, x, c: (pair(y, c), pair(x, c), c))
SWAP = seq_perm(lambda y, x, c: (y, x, 1 - c))


def send(a, pairs):
    return lax.ppermute(a, "seq", pairs)


def gather_keyval(own):
    up, down = send(own, A_UP), send(own, A_DOWN)
    far = jnp.stack([send(up[0], A_UP), send(down[1], A_DOWN)])
    line = jnp.stack([own, up, down, far], axis=1)
    up2, down2 = send(line, B_UP), send(line, B_DOWN)
    far_k, far_v = send(up2[0], B_UP), send(down2[1], B_DOWN)
    mine = [line, up2, down2, far_k, far_v]
    return mine + [send(a, SWAP) for a in mine]


def shard_slots(seq_index):
    shard = jnp.arange(NY * NX * NC, dtype=jnp.int32)

    def parts(i):
        return i // (NX * NC), (i // NC) % NX, i % NC

    ys, xs, cs = parts(shard)
    y0, x0, c0 = parts(seq_index)
    order = jnp.array([0, 2, 3, 1], jnp.int32)
    in_y, in_x = order[(ys - y0) % NY], order[(xs - x0) % NX]
    first = jnp.where(cs == 0, in_x, in_y)
    second = jnp.where(cs == 0, in_y, in_x)
    return (cs != c0) * 16 + second * 4 + first


def attend_kernel(
    slots_ref, vert_ref, diag_ref, q_ref, kpv_ref, kpd_ref,
    l0, u0, d0, fk0, fv0, l1, u1, d1, fk1, fv1,
    o_ref, kbuf, vbuf, sv_ref, pv_ref, od_ref, tot_ref, sems,
):
    heads, rows, width = q_ref.shape
    blocks = rows // BLK
    per = rows // BLK
    copies = ([], [])
    for side, (line, up, down, fk, fv) in enumerate(((l0, u0, d0, fk0, fv0), (l1, u1, d1, fk1, fv1))):
        for which, buf in enumerate((kbuf, vbuf)):
            for j, src in enumerate((line, up, down, (fk, fv)[which])):
                for i in range(4):
                    piece = src.at[i] if j == 3 else src.at[which, i]
                    slot = side * 16 + j * 4 + i
                    copies[which].append(
                        pltpu.make_async_copy(piece, buf.at[slot], sems.at[which, slot])
                    )
    for c in copies[0] + copies[1]:
        c.start()
    for c in copies[0]:
        c.wait()
    for c in copies[1]:
        c.wait()

    def tile(buf, block):
        return buf[slots_ref[block // per], pl.ds(pl.multiple_of((block % per) * BLK, BLK), BLK), :]

    scale = SCALE / math.sqrt(width)
    nt = (((1,), (1,)), ((), ()))

    def one_head(h, carry):
        verts = [vert_ref[h, c] for c in range(8)]
        k_v = jnp.concatenate([tile(kbuf, v) for v in verts], axis=0)
        sv_ref[...] = lax.dot_general(q_ref[h], k_v, nt, preferred_element_type=jnp.float32)
        kpv = kpv_ref[h]
        for b in range(blocks):
            r = slice(b * BLK, (b + 1) * BLK)
            diags = [diag_ref[h * blocks + b, c] for c in range(8)]
            k_d = jnp.concatenate([tile(kbuf, v) for v in diags], axis=0)
            s_d = lax.dot_general(q_ref[h, r, :], k_d, nt, preferred_element_type=jnp.float32)
            s_v = sv_ref[r, :]
            qpos = b * BLK + lax.broadcasted_iota(jnp.int32, (BLK, 1), 0)
            s_d = jnp.where(kpd_ref[h * blocks + b] <= qpos, s_d, -1e30)
            s_v = jnp.where(kpv <= qpos, s_v, -1e30)
            top = jnp.maximum(
                jnp.max(s_d, axis=1, keepdims=True), jnp.max(s_v, axis=1, keepdims=True)
            )
            p_d = jnp.exp2((s_d - top) * scale)
            p_v = jnp.exp2((s_v - top) * scale)
            tot_ref[r, :] = jnp.sum(p_d, axis=1, keepdims=True) + jnp.sum(
                p_v, axis=1, keepdims=True
            )
            pv_ref[r, :] = p_v.astype(jnp.bfloat16)
            v_d = jnp.concatenate([tile(vbuf, v) for v in diags], axis=0)
            od_ref[r, :] = jnp.dot(
                p_d.astype(jnp.bfloat16), v_d, preferred_element_type=jnp.float32
            )
        v_v = jnp.concatenate([tile(vbuf, v) for v in verts], axis=0)
        o_v = jnp.dot(pv_ref[...], v_v, preferred_element_type=jnp.float32)
        o = ((o_v + od_ref[...]) / tot_ref[...]).astype(jnp.bfloat16)
        lanes = pl.ds(pl.multiple_of(h * width, width), width)
        for b in range(blocks):
            o_ref[b, :, lanes] = o[b * BLK : (b + 1) * BLK]
        return carry

    lax.fori_loop(0, heads, one_head, 0)


def attend(query, pieces, slots, vertical, slash, counts, seq_index):
    heads, rows, width = query.shape
    blocks = rows // BLK
    slot = jnp.arange(8, dtype=jnp.int32)
    first = seq_index * blocks
    vert_live = slot[None, :] < counts[:, 0:1]
    diag = first + jnp.arange(blocks, dtype=jnp.int32)[None, :, None] - slash[:, None, :]
    covered = jnp.any(
        (diag[:, :, :, None] == vertical[:, None, None, :]) & vert_live[:, None, None, :], axis=3
    )
    diag_live = (slot < counts[:, 1:2])[:, None, :] & (diag >= 0) & jnp.logical_not(covered)
    within = jnp.arange(BLK, dtype=jnp.int32)
    kpv = jnp.where(
        vert_live[:, :, None], (vertical - first)[:, :, None] * BLK + within, DEAD
    ).reshape(heads, 1, 8 * BLK)
    kpd = jnp.where(
        diag_live[:, :, :, None], (diag - first)[:, :, :, None] * BLK + within, DEAD
    ).reshape(heads * blocks, 1, 8 * BLK)
    diag = jnp.maximum(diag, 0).reshape(heads * blocks, 8)
    smem = pl.BlockSpec(memory_space=pltpu.SMEM)
    vmem = pl.BlockSpec(memory_space=pltpu.VMEM)
    hbm = pl.BlockSpec(memory_space=pl.ANY)
    f32 = jnp.float32
    return pl.pallas_call(
        attend_kernel,
        out_shape=jax.ShapeDtypeStruct((blocks, BLK, heads * width), jnp.bfloat16),
        in_specs=[smem] * 3 + [vmem] * 3 + [hbm] * len(pieces),
        out_specs=vmem,
        scratch_shapes=[
            pltpu.VMEM((32, rows, width), jnp.bfloat16),
            pltpu.VMEM((32, rows, width), jnp.bfloat16),
            pltpu.VMEM((rows, 8 * BLK), f32),
            pltpu.VMEM((rows, 8 * BLK), jnp.bfloat16),
            pltpu.VMEM((rows, width), f32),
            pltpu.VMEM((rows, 1), f32),
            pltpu.SemaphoreType.DMA((2, 32)),
        ],
        compiler_params=pltpu.CompilerParams(vmem_limit_bytes=24 * 2**20),
        name="attend",
    )(slots, vertical, diag, query, kpv, kpd, *pieces)


def ring(n, step):
    return [(i, (i + step) % n) for i in range(n)]


def gather_weight(own):
    n = lax.axis_size("tp")
    half = own.shape[0] // 2

    def up(a):
        return lax.ppermute(a, "tp", ring(n, 1))

    def down(a):
        return lax.ppermute(a, "tp", ring(n, -1))

    u1, d1 = up(own), down(own)
    u2, d2 = up(u1), down(d1)
    u3, d3 = up(u2), down(d2)
    u4, d4 = up(u3[:half]), down(d3[half:])
    mine = [own, u1, d1, u2, d2, u3, d3, u4, d4]
    return mine + [send(a, SWAP) for a in mine]


def project_kernel(place_ref, *refs):
    rows, weights = refs[:4], refs[4:22]
    o_ref, wbuf, acc, sems = refs[22:]
    n, group, depth = rows[0].shape
    cols = weights[0].shape[1]
    tp, core = place_ref[0], place_ref[1]
    half = depth // 2
    copies = []
    for side in range(2):
        for i in range(9):
            dst = wbuf.at[side, i] if i < 7 else wbuf.at[side, 7, pl.ds((i - 7) * half, half)]
            copies.append(pltpu.make_async_copy(weights[side * 9 + i], dst, sems.at[side * 9 + i]))
    for c in copies:
        c.start()
    steps = (0, -1, 1, -2, 2, -3, 3, 4)
    for i, step in enumerate(steps):
        k = lax.rem(tp + step + n, n)
        a = jnp.concatenate([r[k] for r in rows], axis=0)
        for side in range(2):
            copies[side * 9 + i].wait()
            if i == 7:
                copies[side * 9 + 8].wait()
            part = jnp.dot(a, wbuf[side, i], preferred_element_type=jnp.float32)
            if i == 0:
                acc[side] = part
            else:
                acc[side] += part
    for side in range(2):
        col = pl.ds(pl.multiple_of((core if side == 0 else 1 - core) * cols, cols), cols)
        for r in range(4):
            o_ref[r, :, col] = acc[side, pl.ds(r * group, group), :].astype(jnp.bfloat16)


def project(rows, weights, place):
    n, group, depth = rows[0].shape
    cols = weights[0].shape[1]
    vmem = pl.BlockSpec(memory_space=pltpu.VMEM)
    hbm = pl.BlockSpec(memory_space=pl.ANY)
    return pl.pallas_call(
        project_kernel,
        out_shape=jax.ShapeDtypeStruct((4, group, 2 * cols), jnp.bfloat16),
        in_specs=[pl.BlockSpec(memory_space=pltpu.SMEM)] + [vmem] * 4 + [hbm] * len(weights),
        out_specs=vmem,
        scratch_shapes=[
            pltpu.VMEM((2, n, depth, cols), jnp.bfloat16),
            pltpu.VMEM((2, 4 * group, cols), jnp.float32),
            pltpu.SemaphoreType.DMA((18,)),
        ],
        compiler_params=pltpu.CompilerParams(vmem_limit_bytes=40 * 2**20),
        name="project",
    )(place, *rows, *weights)


def per_device(query, keyval, vert_blocks, slash_offsets, counts, out_weight):
    heads, rows, width = query.shape
    seq_index = lax.axis_index("seq")
    tp_index = lax.axis_index("tp")
    core = seq_index % NC
    x_odd = (seq_index // NC) % 2
    y_odd = (seq_index // (NC * NX)) % 2
    block = y_odd * 2 + x_odd
    cols = out_weight.shape[1] // 8
    kv_head = tp_index // (lax.axis_size("tp") // keyval.shape[1])
    own = lax.dynamic_index_in_dim(keyval, kv_head, 1, keepdims=False)
    pieces = gather_keyval(own)
    weights = gather_weight(
        lax.dynamic_slice_in_dim(out_weight, (block * 2 + core) * cols, cols, 1)
    )

    def mine(a):
        return lax.dynamic_slice_in_dim(a, tp_index * heads, heads, 0)

    attended = attend(
        query, pieces, shard_slots(seq_index), mine(vert_blocks), mine(slash_offsets),
        mine(counts), seq_index,
    )
    tokens = lax.all_to_all(attended, "tp", split_axis=0, concat_axis=0, tiled=True)
    moves = (PAIR_X, PAIR_Y, PAIR_XY)
    out = project(
        [tokens] + [send(tokens, m) for m in moves], weights, jnp.stack([tp_index, core])
    )
    back = [out[0]] + [send(out[i + 1], m) for i, m in enumerate(moves)]
    odd_x, odd_y = x_odd == 1, y_odd == 1
    left = [jnp.where(odd_x, back[i ^ 1], back[i]) for i in range(4)]
    return jnp.concatenate([jnp.where(odd_y, left[i ^ 2], left[i]) for i in range(4)], axis=1)


def solution(mesh):
    return jax.shard_map(
        per_device,
        mesh=mesh,
        in_specs=(P("tp", "seq", None), P(None, None, "seq", None), P(), P(), P(), P("tp", None)),
        out_specs=P(("seq", "tp"), None),
        check_vma=False,
    )
```

```python
import functools
import math

import jax
import jax.numpy as jnp
from jax import lax
from jax.experimental import pallas as pl
from jax.experimental.pallas import tpu as pltpu
from jax.sharding import PartitionSpec as P

BLK = 64
NY, NX, NC = 4, 4, 2
DEAD = 1 << 20
SCALE = math.log2(math.e)


def seq_perm(move):
    pairs = []
    for y in range(NY):
        for x in range(NX):
            for c in range(NC):
                ty, tx, tc = move(y, x, c)
                pairs.append(((y * NX + x) * NC + c, ((ty % NY) * NX + tx % NX) * NC + tc))
    return pairs


A_UP = seq_perm(lambda y, x, c: (y, x + 1, c) if c == 0 else (y + 1, x, c))
A_DOWN = seq_perm(lambda y, x, c: (y, x - 1, c) if c == 0 else (y - 1, x, c))
B_UP = seq_perm(lambda y, x, c: (y + 1, x, c) if c == 0 else (y, x + 1, c))
B_DOWN = seq_perm(lambda y, x, c: (y - 1, x, c) if c == 0 else (y, x - 1, c))
def pair(v, c):
    return (v ^ 1) if c == 0 else (v + 1 if v % 2 else v - 1)


PAIR_X = seq_perm(lambda y, x, c: (y, pair(x, c), c))
PAIR_Y = seq_perm(lambda y, x, c: (pair(y, c), x, c))
PAIR_XY = seq_perm(lambda y, x, c: (pair(y, c), pair(x, c), c))
SWAP = seq_perm(lambda y, x, c: (y, x, 1 - c))


def send(a, pairs):
    return lax.ppermute(a, "seq", pairs)


def gather_keyval(own):
    up, down = send(own, A_UP), send(own, A_DOWN)
    far = jnp.stack([send(up[0], A_UP), send(down[1], A_DOWN)])
    line = jnp.stack([own, up, down, far], axis=1)
    up2, down2 = send(line, B_UP), send(line, B_DOWN)
    far_k, far_v = send(up2[0], B_UP), send(down2[1], B_DOWN)
    mine = [line, up2, down2, far_k, far_v]
    return mine + [send(a, SWAP) for a in mine]


def shard_slots(seq_index):
    shard = jnp.arange(NY * NX * NC, dtype=jnp.int32)

    def parts(i):
        return i // (NX * NC), (i // NC) % NX, i % NC

    ys, xs, cs = parts(shard)
    y0, x0, c0 = parts(seq_index)
    order = jnp.array([0, 2, 3, 1], jnp.int32)
    in_y, in_x = order[(ys - y0) % NY], order[(xs - x0) % NX]
    first = jnp.where(cs == 0, in_x, in_y)
    second = jnp.where(cs == 0, in_y, in_x)
    return (cs != c0) * 16 + second * 4 + first


def attend_kernel(
    slots_ref, vert_ref, diag_ref, q_ref, kpv_ref, kpd_ref,
    l0, u0, d0, fk0, fv0, l1, u1, d1, fk1, fv1,
    o_ref, kbuf, vbuf, sv_ref, pv_ref, od_ref, tot_ref, sems,
):
    heads, rows, width = q_ref.shape
    blocks = rows // BLK
    per = rows // BLK
    copies = ([], [])
    for side, (line, up, down, fk, fv) in enumerate(((l0, u0, d0, fk0, fv0), (l1, u1, d1, fk1, fv1))):
        for which, buf in enumerate((kbuf, vbuf)):
            for j, src in enumerate((line, up, down, (fk, fv)[which])):
                for i in range(4):
                    piece = src.at[i] if j == 3 else src.at[which, i]
                    slot = side * 16 + j * 4 + i
                    copies[which].append(
                        pltpu.make_async_copy(piece, buf.at[slot], sems.at[which, slot])
                    )
    for c in copies[0] + copies[1]:
        c.start()
    for c in copies[0]:
        c.wait()
    for c in copies[1]:
        c.wait()

    def tile(buf, block):
        return buf[slots_ref[block // per], pl.ds(pl.multiple_of((block % per) * BLK, BLK), BLK), :]

    scale = SCALE / math.sqrt(width)
    nt = (((1,), (1,)), ((), ()))

    def one_head(h, carry):
        verts = [vert_ref[h, c] for c in range(8)]
        k_v = jnp.concatenate([tile(kbuf, v) for v in verts], axis=0)
        sv_ref[...] = lax.dot_general(q_ref[h], k_v, nt, preferred_element_type=jnp.float32)
        kpv = kpv_ref[h]
        for b in range(blocks):
            r = slice(b * BLK, (b + 1) * BLK)
            diags = [diag_ref[h * blocks + b, c] for c in range(8)]
            k_d = jnp.concatenate([tile(kbuf, v) for v in diags], axis=0)
            s_d = lax.dot_general(q_ref[h, r, :], k_d, nt, preferred_element_type=jnp.float32)
            s_v = sv_ref[r, :]
            qpos = b * BLK + lax.broadcasted_iota(jnp.int32, (BLK, 1), 0)
            s_d = jnp.where(kpd_ref[h * blocks + b] <= qpos, s_d, -1e30)
            s_v = jnp.where(kpv <= qpos, s_v, -1e30)
            top = jnp.maximum(
                jnp.max(s_d, axis=1, keepdims=True), jnp.max(s_v, axis=1, keepdims=True)
            )
            p_d = jnp.exp2((s_d - top) * scale)
            p_v = jnp.exp2((s_v - top) * scale)
            tot_ref[r, :] = jnp.sum(p_d, axis=1, keepdims=True) + jnp.sum(
                p_v, axis=1, keepdims=True
            )
            pv_ref[r, :] = p_v.astype(jnp.bfloat16)
            v_d = jnp.concatenate([tile(vbuf, v) for v in diags], axis=0)
            od_ref[r, :] = jnp.dot(
                p_d.astype(jnp.bfloat16), v_d, preferred_element_type=jnp.float32
            )
        v_v = jnp.concatenate([tile(vbuf, v) for v in verts], axis=0)
        o_v = jnp.dot(pv_ref[...], v_v, preferred_element_type=jnp.float32)
        o = ((o_v + od_ref[...]) / tot_ref[...]).astype(jnp.bfloat16)
        lanes = pl.ds(pl.multiple_of(h * width, width), width)
        for b in range(blocks):
            o_ref[b, :, lanes] = o[b * BLK : (b + 1) * BLK]
        return carry

    lax.fori_loop(0, heads, one_head, 0)


def attend(query, pieces, slots, vertical, slash, counts, seq_index):
    heads, rows, width = query.shape
    blocks = rows // BLK
    slot = jnp.arange(8, dtype=jnp.int32)
    first = seq_index * blocks
    vert_live = slot[None, :] < counts[:, 0:1]
    diag = first + jnp.arange(blocks, dtype=jnp.int32)[None, :, None] - slash[:, None, :]
    covered = jnp.any(
        (diag[:, :, :, None] == vertical[:, None, None, :]) & vert_live[:, None, None, :], axis=3
    )
    diag_live = (slot < counts[:, 1:2])[:, None, :] & (diag >= 0) & jnp.logical_not(covered)
    within = jnp.arange(BLK, dtype=jnp.int32)
    kpv = jnp.where(
        vert_live[:, :, None], (vertical - first)[:, :, None] * BLK + within, DEAD
    ).reshape(heads, 1, 8 * BLK)
    kpd = jnp.where(
        diag_live[:, :, :, None], (diag - first)[:, :, :, None] * BLK + within, DEAD
    ).reshape(heads * blocks, 1, 8 * BLK)
    diag = jnp.maximum(diag, 0).reshape(heads * blocks, 8)
    smem = pl.BlockSpec(memory_space=pltpu.SMEM)
    vmem = pl.BlockSpec(memory_space=pltpu.VMEM)
    hbm = pl.BlockSpec(memory_space=pl.ANY)
    f32 = jnp.float32
    return pl.pallas_call(
        attend_kernel,
        out_shape=jax.ShapeDtypeStruct((blocks, BLK, heads * width), jnp.bfloat16),
        in_specs=[smem] * 3 + [vmem] * 3 + [hbm] * len(pieces),
        out_specs=vmem,
        scratch_shapes=[
            pltpu.VMEM((32, rows, width), jnp.bfloat16),
            pltpu.VMEM((32, rows, width), jnp.bfloat16),
            pltpu.VMEM((rows, 8 * BLK), f32),
            pltpu.VMEM((rows, 8 * BLK), jnp.bfloat16),
            pltpu.VMEM((rows, width), f32),
            pltpu.VMEM((rows, 1), f32),
            pltpu.SemaphoreType.DMA((2, 32)),
        ],
        compiler_params=pltpu.CompilerParams(vmem_limit_bytes=24 * 2**20),
        cost_estimate=pl.CostEstimate(flops=2**31, bytes_accessed=48 * 2**20, transcendentals=2**21),
        name="attend",
    )(slots, vertical, diag, query, kpv, kpd, *pieces)


def ring(n, step):
    return [(i, (i + step) % n) for i in range(n)]


def after(arrays, dep):
    count = len(arrays)
    hbm = pl.BlockSpec(memory_space=pl.ANY)
    return pl.pallas_call(
        lambda *refs: None,
        out_shape=[jax.ShapeDtypeStruct(a.shape, a.dtype) for a in arrays],
        in_specs=[hbm] * (count + 1),
        out_specs=[hbm] * count,
        input_output_aliases={i: i for i in range(count)},
        name="after",
    )(*arrays, dep)


def up(a):
    return lax.ppermute(a, "tp", ring(lax.axis_size("tp"), 1))


def down(a):
    return lax.ppermute(a, "tp", ring(lax.axis_size("tp"), -1))


def project_kernel(place_ref, *refs):
    rows, weights = refs[:8], refs[8:17]
    mine_ref, theirs_ref, wbuf, acc, sems = refs[17:]
    n, group, depth = rows[0].shape
    tp = place_ref[0]
    half = depth // 2
    copies = []
    for i in range(9):
        dst = wbuf.at[i] if i < 7 else wbuf.at[7, pl.ds((i - 7) * half, half)]
        copies.append(pltpu.make_async_copy(weights[i], dst, sems.at[i]))
    for c in copies:
        c.start()
    for i, step in enumerate((0, -1, 1, -2, 2, -3, 3, 4)):
        k = lax.rem(tp + step + n, n)
        a = jnp.concatenate([r[k] for r in rows], axis=0)
        copies[i].wait()
        if i == 7:
            copies[8].wait()
        part = jnp.dot(a, wbuf[i], preferred_element_type=jnp.float32)
        if i == 0:
            acc[...] = part
        else:
            acc[...] += part
    for r in range(4):
        mine_ref[r] = acc[pl.ds(r * group, group), :].astype(jnp.bfloat16)
        theirs_ref[r] = acc[pl.ds((r + 4) * group, group), :].astype(jnp.bfloat16)


def project(rows, weights, place):
    n, group, depth = rows[0].shape
    cols = weights[0].shape[1]
    vmem = pl.BlockSpec(memory_space=pltpu.VMEM)
    hbm = pl.BlockSpec(memory_space=pl.ANY)
    return pl.pallas_call(
        project_kernel,
        out_shape=[jax.ShapeDtypeStruct((4, group, cols), jnp.bfloat16)] * 2,
        in_specs=[pl.BlockSpec(memory_space=pltpu.SMEM)] + [vmem] * 8 + [hbm] * 9,
        out_specs=[vmem] * 2,
        scratch_shapes=[
            pltpu.VMEM((n, depth, cols), jnp.bfloat16),
            pltpu.VMEM((8 * group, cols), jnp.float32),
            pltpu.SemaphoreType.DMA((9,)),
        ],
        compiler_params=pltpu.CompilerParams(vmem_limit_bytes=32 * 2**20),
        cost_estimate=pl.CostEstimate(flops=2**32, bytes_accessed=2**24, transcendentals=0),
        name="project",
    )(place, *rows, *weights)


def per_device(query, keyval, vert_blocks, slash_offsets, counts, out_weight):
    heads, rows, width = query.shape
    seq_index = lax.axis_index("seq")
    tp_index = lax.axis_index("tp")
    core = seq_index % NC
    x_odd = (seq_index // NC) % 2
    y_odd = (seq_index // (NC * NX)) % 2
    block = y_odd * 2 + x_odd
    cols = out_weight.shape[1] // 8
    depth = out_weight.shape[0] // 2
    kv_head = tp_index // (lax.axis_size("tp") // keyval.shape[1])
    own = lax.dynamic_index_in_dim(keyval, kv_head, 1, keepdims=False)
    w0 = lax.dynamic_slice_in_dim(out_weight, (block * 2 + core) * cols, cols, 1)

    up_a, down_a = send(own, A_UP), send(own, A_DOWN)
    w_u1, w_d1 = up(w0), down(w0)
    far = jnp.stack([send(up_a[0], A_UP), send(down_a[1], A_DOWN)])
    line = jnp.stack([own, up_a, down_a, far], axis=1)
    up_b, down_b = send(line, B_UP), send(line, B_DOWN)
    far_k, far_v = send(up_b[0], B_UP), send(down_b[1], B_DOWN)
    w_u1, w_d1 = after([w_u1, w_d1], down_b)
    w_u2, w_d2 = up(w_u1), down(w_d1)
    pieces = [line, up_b, down_b, far_k, far_v]
    pieces += [send(a, SWAP) for a in pieces]

    def mine(a):
        return lax.dynamic_slice_in_dim(a, tp_index * heads, heads, 0)

    attended = attend(
        query, pieces, shard_slots(seq_index), mine(vert_blocks), mine(slash_offsets),
        mine(counts), seq_index,
    )
    w_u2, w_d2 = after([w_u2, w_d2], attended)
    w_u3, w_d3 = up(w_u2), down(w_d2)
    tokens = lax.all_to_all(attended, "tp", split_axis=0, concat_axis=0, tiled=True)
    w_u3, w_d3 = after([w_u3, w_d3], tokens)
    w_u4, w_d4 = up(w_u3[:depth]), down(w_d3[depth:])
    moves = (PAIR_X, PAIR_Y, PAIR_XY)
    group = [tokens] + [send(tokens, m) for m in moves]
    group += [send(a, SWAP) for a in group]
    ours, theirs = project(
        group, [w0, w_u1, w_d1, w_u2, w_d2, w_u3, w_d3, w_u4, w_d4], jnp.stack([tp_index, core])
    )
    other = send(theirs, SWAP)
    out = jnp.concatenate(
        [jnp.where(core == 0, ours, other), jnp.where(core == 0, other, ours)], axis=2
    )
    back = [out[0]] + [send(out[i + 1], m) for i, m in enumerate(moves)]
    odd_x, odd_y = x_odd == 1, y_odd == 1
    left = [jnp.where(odd_x, back[i ^ 1], back[i]) for i in range(4)]
    return jnp.concatenate([jnp.where(odd_y, left[i ^ 2], left[i]) for i in range(4)], axis=1)


def solution(mesh):
    return jax.shard_map(
        per_device,
        mesh=mesh,
        in_specs=(P("tp", "seq", None), P(None, None, "seq", None), P(), P(), P(), P("tp", None)),
        out_specs=P(("seq", "tp"), None),
        check_vma=False,
    )
```

```python
import functools
import math

import jax
import jax.numpy as jnp
from jax import lax
from jax.experimental import pallas as pl
from jax.experimental.pallas import tpu as pltpu
from jax.sharding import PartitionSpec as P

BLK = 64
NY, NX, NC = 4, 4, 2
DEAD = 1 << 20
SCALE = math.log2(math.e)


def seq_perm(move):
    pairs = []
    for y in range(NY):
        for x in range(NX):
            for c in range(NC):
                ty, tx, tc = move(y, x, c)
                pairs.append(((y * NX + x) * NC + c, ((ty % NY) * NX + tx % NX) * NC + tc))
    return pairs


A_UP = seq_perm(lambda y, x, c: (y, x + 1, c) if c == 0 else (y + 1, x, c))
A_DOWN = seq_perm(lambda y, x, c: (y, x - 1, c) if c == 0 else (y - 1, x, c))
B_UP = seq_perm(lambda y, x, c: (y + 1, x, c) if c == 0 else (y, x + 1, c))
B_DOWN = seq_perm(lambda y, x, c: (y - 1, x, c) if c == 0 else (y, x - 1, c))
def pair(v, c):
    return (v ^ 1) if c == 0 else (v + 1 if v % 2 else v - 1)


PAIR_X = seq_perm(lambda y, x, c: (y, pair(x, c), c))
PAIR_Y = seq_perm(lambda y, x, c: (pair(y, c), x, c))
PAIR_XY = seq_perm(lambda y, x, c: (pair(y, c), pair(x, c), c))
SWAP = seq_perm(lambda y, x, c: (y, x, 1 - c))


def send(a, pairs):
    return lax.ppermute(a, "seq", pairs)


def gather_keyval(own):
    up, down = send(own, A_UP), send(own, A_DOWN)
    far = jnp.stack([send(up[0], A_UP), send(down[1], A_DOWN)])
    line = jnp.stack([own, up, down, far], axis=1)
    up2, down2 = send(line, B_UP), send(line, B_DOWN)
    far_k, far_v = send(up2[0], B_UP), send(down2[1], B_DOWN)
    mine = [line, up2, down2, far_k, far_v]
    return mine + [send(a, SWAP) for a in mine]


def shard_slots(seq_index):
    shard = jnp.arange(NY * NX * NC, dtype=jnp.int32)

    def parts(i):
        return i // (NX * NC), (i // NC) % NX, i % NC

    ys, xs, cs = parts(shard)
    y0, x0, c0 = parts(seq_index)
    order = jnp.array([0, 2, 3, 1], jnp.int32)
    in_y, in_x = order[(ys - y0) % NY], order[(xs - x0) % NX]
    first = jnp.where(cs == 0, in_x, in_y)
    second = jnp.where(cs == 0, in_y, in_x)
    return (cs != c0) * 16 + second * 4 + first


def attend_kernel(
    slots_ref, vert_ref, diag_ref, q_ref, kpv_ref, kpd_ref,
    l0, u0, d0, fk0, fv0, l1, u1, d1, fk1, fv1,
    o_ref, kbuf, vbuf, sv_ref, sd_ref, pv_ref, pd_ref, tot_ref, sems,
):
    heads, rows, width = q_ref.shape
    blocks = rows // BLK
    per = rows // BLK
    copies = ([], [])
    for side, (line, up, down, fk, fv) in enumerate(((l0, u0, d0, fk0, fv0), (l1, u1, d1, fk1, fv1))):
        for which, buf in enumerate((kbuf, vbuf)):
            for j, src in enumerate((line, up, down, (fk, fv)[which])):
                slot = side * 16 + j * 4
                copies[which].append(
                    pltpu.make_async_copy(
                        src if j == 3 else src.at[which],
                        buf.at[pl.ds(slot, 4)],
                        sems.at[which, side * 4 + j],
                    )
                )
    for c in copies[0] + copies[1]:
        c.start()
    for c in copies[0]:
        c.wait()

    def tile(buf, block):
        return buf[slots_ref[block // per], pl.ds(pl.multiple_of((block % per) * BLK, BLK), BLK), :]

    scale = SCALE / math.sqrt(width)
    nt = (((1,), (1,)), ((), ()))

    def one_head(h):
        verts = [vert_ref[h, c] for c in range(8)]
        diags = [[diag_ref[h * blocks + b, c] for c in range(8)] for b in range(blocks)]
        sv, sd, pv, pd, tot = (r.at[h % 2] for r in (sv_ref, sd_ref, pv_ref, pd_ref, tot_ref))
        k_v = jnp.concatenate([tile(kbuf, v) for v in verts], axis=0)
        sv[...] = lax.dot_general(q_ref[h], k_v, nt, preferred_element_type=jnp.float32)
        for b in range(blocks):
            r = slice(b * BLK, (b + 1) * BLK)
            k_d = jnp.concatenate([tile(kbuf, v) for v in diags[b]], axis=0)
            sd[r, :] = lax.dot_general(q_ref[h, r, :], k_d, nt, preferred_element_type=jnp.float32)
        kpv = kpv_ref[h]
        for b in range(blocks):
            r = slice(b * BLK, (b + 1) * BLK)
            qpos = b * BLK + lax.broadcasted_iota(jnp.int32, (BLK, 1), 0)
            s_d = jnp.where(kpd_ref[h * blocks + b] <= qpos, sd[r, :], -1e30)
            s_v = jnp.where(kpv <= qpos, sv[r, :], -1e30)
            top = jnp.maximum(
                jnp.max(s_d, axis=1, keepdims=True), jnp.max(s_v, axis=1, keepdims=True)
            )
            p_d = jnp.exp2((s_d - top) * scale)
            p_v = jnp.exp2((s_v - top) * scale)
            tot[r, :] = jnp.sum(p_d, axis=1, keepdims=True) + jnp.sum(p_v, axis=1, keepdims=True)
            pv[r, :] = p_v.astype(jnp.bfloat16)
            pd[r, :] = p_d.astype(jnp.bfloat16)
        if h == 0:
            for c in copies[1]:
                c.wait()
        v_v = jnp.concatenate([tile(vbuf, v) for v in verts], axis=0)
        o_v = jnp.dot(pv[...], v_v, preferred_element_type=jnp.float32)
        for b in range(blocks):
            r = slice(b * BLK, (b + 1) * BLK)
            v_d = jnp.concatenate([tile(vbuf, v) for v in diags[b]], axis=0)
            o_d = jnp.dot(pd[r, :], v_d, preferred_element_type=jnp.float32)
            o = ((o_v[r] + o_d) / tot[r, :]).astype(jnp.bfloat16)
            o_ref[b, :, h * width : (h + 1) * width] = o

    for h in range(heads):
        one_head(h)


def attend(query, pieces, slots, vertical, slash, counts, seq_index):
    heads, rows, width = query.shape
    blocks = rows // BLK
    slot = jnp.arange(8, dtype=jnp.int32)
    first = seq_index * blocks
    vert_live = slot[None, :] < counts[:, 0:1]
    diag = first + jnp.arange(blocks, dtype=jnp.int32)[None, :, None] - slash[:, None, :]
    covered = jnp.any(
        (diag[:, :, :, None] == vertical[:, None, None, :]) & vert_live[:, None, None, :], axis=3
    )
    diag_live = (slot < counts[:, 1:2])[:, None, :] & (diag >= 0) & jnp.logical_not(covered)
    within = jnp.arange(BLK, dtype=jnp.int32)
    kpv = jnp.where(
        vert_live[:, :, None], (vertical - first)[:, :, None] * BLK + within, DEAD
    ).reshape(heads, 1, 8 * BLK)
    kpd = jnp.where(
        diag_live[:, :, :, None], (diag - first)[:, :, :, None] * BLK + within, DEAD
    ).reshape(heads * blocks, 1, 8 * BLK)
    diag = jnp.maximum(diag, 0).reshape(heads * blocks, 8)
    smem = pl.BlockSpec(memory_space=pltpu.SMEM)
    vmem = pl.BlockSpec(memory_space=pltpu.VMEM)
    hbm = pl.BlockSpec(memory_space=pltpu.HBM)
    f32 = jnp.float32
    return pl.pallas_call(
        attend_kernel,
        out_shape=jax.ShapeDtypeStruct((blocks, BLK, heads * width), jnp.bfloat16),
        in_specs=[smem] * 3 + [vmem] * 3 + [hbm] * len(pieces),
        out_specs=vmem,
        scratch_shapes=[
            pltpu.VMEM((32, rows, width), jnp.bfloat16),
            pltpu.VMEM((32, rows, width), jnp.bfloat16),
            pltpu.VMEM((2, rows, 8 * BLK), f32),
            pltpu.VMEM((2, rows, 8 * BLK), f32),
            pltpu.VMEM((2, rows, 8 * BLK), jnp.bfloat16),
            pltpu.VMEM((2, rows, 8 * BLK), jnp.bfloat16),
            pltpu.VMEM((2, rows, 1), f32),
            pltpu.SemaphoreType.DMA((2, 8)),
        ],
        compiler_params=pltpu.CompilerParams(vmem_limit_bytes=24 * 2**20),
        cost_estimate=pl.CostEstimate(flops=2**31, bytes_accessed=24 * 2**20, transcendentals=2**21),
        name="attend",
    )(slots, vertical, diag, query, kpv, kpd, *pieces)


def ring(n, step):
    return [(i, (i + step) % n) for i in range(n)]


def after(arrays, dep):
    count = len(arrays)
    hbm = pl.BlockSpec(memory_space=pltpu.HBM)
    return pl.pallas_call(
        lambda *refs: None,
        out_shape=[jax.ShapeDtypeStruct(a.shape, a.dtype) for a in arrays],
        in_specs=[hbm] * (count + 1),
        out_specs=[hbm] * count,
        input_output_aliases={i: i for i in range(count)},
        name="after",
    )(*arrays, dep)


def up(a):
    return lax.ppermute(a, "tp", ring(lax.axis_size("tp"), 1))


def down(a):
    return lax.ppermute(a, "tp", ring(lax.axis_size("tp"), -1))


def project_kernel(place_ref, *refs):
    rows, weights = refs[:8], refs[8:17]
    mine_ref, theirs_ref, wbuf, acc, sems = refs[17:]
    n, group, depth = rows[0].shape
    tp = place_ref[0]
    half = depth // 2
    copies = []
    for i in range(9):
        dst = wbuf.at[i] if i < 7 else wbuf.at[7, pl.ds((i - 7) * half, half)]
        copies.append(pltpu.make_async_copy(weights[i], dst, sems.at[i]))
    for c in copies:
        c.start()
    for i, step in enumerate((0, -1, 1, -2, 2, -3, 3, 4)):
        k = lax.rem(tp + step + n, n)
        a = jnp.concatenate([r[k] for r in rows], axis=0)
        copies[i].wait()
        if i == 7:
            copies[8].wait()
        part = jnp.dot(a, wbuf[i], preferred_element_type=jnp.float32)
        if i == 0:
            acc[...] = part
        else:
            acc[...] += part
    for r in range(4):
        mine_ref[r] = acc[pl.ds(r * group, group), :].astype(jnp.bfloat16)
        theirs_ref[r] = acc[pl.ds((r + 4) * group, group), :].astype(jnp.bfloat16)


def project(rows, weights, place):
    n, group, depth = rows[0].shape
    cols = weights[0].shape[1]
    vmem = pl.BlockSpec(memory_space=pltpu.VMEM)
    hbm = pl.BlockSpec(memory_space=pltpu.HBM)
    return pl.pallas_call(
        project_kernel,
        out_shape=[jax.ShapeDtypeStruct((4, group, cols), jnp.bfloat16)] * 2,
        in_specs=[pl.BlockSpec(memory_space=pltpu.SMEM)] + [vmem] * 8 + [hbm] * 9,
        out_specs=[vmem] * 2,
        scratch_shapes=[
            pltpu.VMEM((n, depth, cols), jnp.bfloat16),
            pltpu.VMEM((8 * group, cols), jnp.float32),
            pltpu.SemaphoreType.DMA((9,)),
        ],
        compiler_params=pltpu.CompilerParams(vmem_limit_bytes=32 * 2**20),
        cost_estimate=pl.CostEstimate(flops=2**32, bytes_accessed=2**24, transcendentals=0),
        name="project",
    )(place, *rows, *weights)


def per_device(query, keyval, vert_blocks, slash_offsets, counts, out_weight):
    heads, rows, width = query.shape
    seq_index = lax.axis_index("seq")
    tp_index = lax.axis_index("tp")
    core = seq_index % NC
    x_odd = (seq_index // NC) % 2
    y_odd = (seq_index // (NC * NX)) % 2
    block = y_odd * 2 + x_odd
    cols = out_weight.shape[1] // 8
    depth = out_weight.shape[0] // 2
    kv_head = tp_index // (lax.axis_size("tp") // keyval.shape[1])
    own = lax.dynamic_index_in_dim(keyval, kv_head, 1, keepdims=False)
    w0 = lax.dynamic_slice_in_dim(out_weight, (block * 2 + core) * cols, cols, 1)

    up_a, down_a = send(own, A_UP), send(own, A_DOWN)
    w_u1, w_d1 = up(w0), down(w0)
    up_a, down_a = after([up_a, down_a], w0)
    far = jnp.stack([send(up_a[0], A_UP), send(down_a[1], A_DOWN)])
    line = jnp.stack([own, up_a, down_a, far], axis=1)
    up_b, down_b = send(line, B_UP), send(line, B_DOWN)
    far_k, far_v = send(up_b[0], B_UP), send(down_b[1], B_DOWN)
    pieces = [line, up_b, down_b, far_k, far_v]
    pieces += [send(a, SWAP) for a in pieces]
    w_u1, w_d1 = after([w_u1, w_d1], pieces[5])
    w_u2, w_d2 = up(w_u1), down(w_d1)

    def mine(a):
        return lax.dynamic_slice_in_dim(a, tp_index * heads, heads, 0)

    attended = attend(
        query, pieces, shard_slots(seq_index), mine(vert_blocks), mine(slash_offsets),
        mine(counts), seq_index,
    )
    w_u2, w_d2 = after([w_u2, w_d2], attended)
    w_u3, w_d3 = up(w_u2), down(w_d2)
    tokens = lax.all_to_all(attended, "tp", split_axis=0, concat_axis=0, tiled=True)
    w_u3, w_d3 = after([w_u3, w_d3], tokens)
    w_u4, w_d4 = up(w_u3[:depth]), down(w_d3[depth:])
    moves = (PAIR_X, PAIR_Y, PAIR_XY)
    group = [tokens] + [send(tokens, m) for m in moves]
    group += [send(a, SWAP) for a in group]
    ours, theirs = project(
        group, [w0, w_u1, w_d1, w_u2, w_d2, w_u3, w_d3, w_u4, w_d4], jnp.stack([tp_index, core])
    )
    other = send(theirs, SWAP)
    out = jnp.concatenate(
        [jnp.where(core == 0, ours, other), jnp.where(core == 0, other, ours)], axis=2
    )
    back = [out[0]] + [send(out[i + 1], m) for i, m in enumerate(moves)]
    odd_x, odd_y = x_odd == 1, y_odd == 1
    left = [jnp.where(odd_x, back[i ^ 1], back[i]) for i in range(4)]
    return jnp.concatenate([jnp.where(odd_y, left[i ^ 2], left[i]) for i in range(4)], axis=1)


def solution(mesh):
    return jax.shard_map(
        per_device,
        mesh=mesh,
        in_specs=(P("tp", "seq", None), P(None, None, "seq", None), P(), P(), P(), P("tp", None)),
        out_specs=P(("seq", "tp"), None),
        check_vma=False,
    )
```

```python
import functools
import math

import jax
import jax.numpy as jnp
from jax import lax
from jax.experimental import pallas as pl
from jax.experimental.pallas import tpu as pltpu
from jax.sharding import PartitionSpec as P

BLK = 64
NY, NX, NC = 4, 4, 2
DEAD = 1 << 20
SCALE = math.log2(math.e)


def seq_perm(move):
    pairs = []
    for y in range(NY):
        for x in range(NX):
            for c in range(NC):
                ty, tx, tc = move(y, x, c)
                pairs.append(((y * NX + x) * NC + c, ((ty % NY) * NX + tx % NX) * NC + tc))
    return pairs


A_UP = seq_perm(lambda y, x, c: (y, x + 1, c) if c == 0 else (y + 1, x, c))
A_DOWN = seq_perm(lambda y, x, c: (y, x - 1, c) if c == 0 else (y - 1, x, c))
A_FAR = seq_perm(lambda y, x, c: (y, x + 2, c) if c == 0 else (y + 2, x, c))
B_UP = seq_perm(lambda y, x, c: (y + 1, x, c) if c == 0 else (y, x + 1, c))
B_DOWN = seq_perm(lambda y, x, c: (y - 1, x, c) if c == 0 else (y, x - 1, c))
def pair(v, c):
    return (v ^ 1) if c == 0 else (v + 1 if v % 2 else v - 1)


def partner(r, other):
    return seq_perm(
        lambda y, x, c: (
            pair(y, c ^ other) if r & 2 else y,
            pair(x, c ^ other) if r & 1 else x,
            c ^ other,
        )
    )


SWAP = seq_perm(lambda y, x, c: (y, x, 1 - c))


def send(a, pairs):
    return lax.ppermute(a, "seq", pairs)


def shard_slots(seq_index):
    shard = jnp.arange(NY * NX * NC, dtype=jnp.int32)

    def parts(i):
        return i // (NX * NC), (i // NC) % NX, i % NC

    ys, xs, cs = parts(shard)
    y0, x0, c0 = parts(seq_index)
    order = jnp.array([0, 2, 3, 1], jnp.int32)
    in_y, in_x = order[(ys - y0) % NY], order[(xs - x0) % NX]
    first = jnp.where(cs == 0, in_x, in_y)
    second = jnp.where(cs == 0, in_y, in_x)
    return (cs != c0) * 16 + second * 4 + first


def attend_kernel(slots_ref, vert_ref, diag_ref, q_ref, kpv_ref, kpd_ref, *refs):
    pieces, o_ref = refs[:14], refs[14]
    kbuf, vbuf, sv_ref, sd_ref, pv_ref, pd_ref, tot_ref, sems = refs[15:]
    heads, rows, width = q_ref.shape
    blocks = rows // BLK
    per = rows // BLK
    copies = ([], [])
    for side in range(2):
        line, *rest = pieces[side * 7 : side * 7 + 7]
        for which, buf in enumerate((kbuf, vbuf)):
            for j, src in enumerate([line.at[which]] + rest[which * 3 : which * 3 + 3]):
                copies[which].append(
                    pltpu.make_async_copy(
                        src, buf.at[pl.ds(side * 16 + j * 4, 4)], sems.at[which, side * 4 + j]
                    )
                )
    for c in copies[0] + copies[1]:
        c.start()
    for c in copies[0]:
        c.wait()

    def tile(buf, block):
        return buf[slots_ref[block // per], pl.ds(pl.multiple_of((block % per) * BLK, BLK), BLK), :]

    scale = SCALE / math.sqrt(width)
    nt = (((1,), (1,)), ((), ()))

    def one_head(h):
        verts = [vert_ref[h, c] for c in range(8)]
        diags = [[diag_ref[h * blocks + b, c] for c in range(8)] for b in range(blocks)]
        sv, sd, pv, pd, tot = (r.at[h % 2] for r in (sv_ref, sd_ref, pv_ref, pd_ref, tot_ref))
        k_v = jnp.concatenate([tile(kbuf, v) for v in verts], axis=0)
        sv[...] = lax.dot_general(q_ref[h], k_v, nt, preferred_element_type=jnp.float32)
        for b in range(blocks):
            r = slice(b * BLK, (b + 1) * BLK)
            k_d = jnp.concatenate([tile(kbuf, v) for v in diags[b]], axis=0)
            sd[r, :] = lax.dot_general(q_ref[h, r, :], k_d, nt, preferred_element_type=jnp.float32)
        kpv = kpv_ref[h]
        for b in range(blocks):
            r = slice(b * BLK, (b + 1) * BLK)
            qpos = b * BLK + lax.broadcasted_iota(jnp.int32, (BLK, 1), 0)
            s_d = jnp.where(kpd_ref[h * blocks + b] <= qpos, sd[r, :], -1e30)
            s_v = jnp.where(kpv <= qpos, sv[r, :], -1e30)
            top = jnp.maximum(
                jnp.max(s_d, axis=1, keepdims=True), jnp.max(s_v, axis=1, keepdims=True)
            )
            p_d = jnp.exp2((s_d - top) * scale)
            p_v = jnp.exp2((s_v - top) * scale)
            tot[r, :] = jnp.sum(p_d, axis=1, keepdims=True) + jnp.sum(p_v, axis=1, keepdims=True)
            pv[r, :] = p_v.astype(jnp.bfloat16)
            pd[r, :] = p_d.astype(jnp.bfloat16)
        if h == 0:
            for c in copies[1]:
                c.wait()
        v_v = jnp.concatenate([tile(vbuf, v) for v in verts], axis=0)
        o_v = jnp.dot(pv[...], v_v, preferred_element_type=jnp.float32)
        for b in range(blocks):
            r = slice(b * BLK, (b + 1) * BLK)
            v_d = jnp.concatenate([tile(vbuf, v) for v in diags[b]], axis=0)
            o_d = jnp.dot(pd[r, :], v_d, preferred_element_type=jnp.float32)
            o = ((o_v[r] + o_d) / tot[r, :]).astype(jnp.bfloat16)
            o_ref[b, :, h * width : (h + 1) * width] = o

    for h in range(heads):
        one_head(h)


def attend(query, pieces, slots, vertical, slash, counts, seq_index):
    heads, rows, width = query.shape
    blocks = rows // BLK
    slot = jnp.arange(8, dtype=jnp.int32)
    first = seq_index * blocks
    vert_live = slot[None, :] < counts[:, 0:1]
    diag = first + jnp.arange(blocks, dtype=jnp.int32)[None, :, None] - slash[:, None, :]
    covered = jnp.any(
        (diag[:, :, :, None] == vertical[:, None, None, :]) & vert_live[:, None, None, :], axis=3
    )
    diag_live = (slot < counts[:, 1:2])[:, None, :] & (diag >= 0) & jnp.logical_not(covered)
    within = jnp.arange(BLK, dtype=jnp.int32)
    kpv = jnp.where(
        vert_live[:, :, None], (vertical - first)[:, :, None] * BLK + within, DEAD
    ).reshape(heads, 1, 8 * BLK)
    kpd = jnp.where(
        diag_live[:, :, :, None], (diag - first)[:, :, :, None] * BLK + within, DEAD
    ).reshape(heads * blocks, 1, 8 * BLK)
    diag = jnp.maximum(diag, 0).reshape(heads * blocks, 8)
    smem = pl.BlockSpec(memory_space=pltpu.SMEM)
    vmem = pl.BlockSpec(memory_space=pltpu.VMEM)
    hbm = pl.BlockSpec(memory_space=pl.ANY)
    f32 = jnp.float32
    return pl.pallas_call(
        attend_kernel,
        out_shape=jax.ShapeDtypeStruct((blocks, BLK, heads * width), jnp.bfloat16),
        in_specs=[smem] * 3 + [vmem] * 3 + [hbm] * len(pieces),
        out_specs=vmem,
        scratch_shapes=[
            pltpu.VMEM((32, rows, width), jnp.bfloat16),
            pltpu.VMEM((32, rows, width), jnp.bfloat16),
            pltpu.VMEM((2, rows, 8 * BLK), f32),
            pltpu.VMEM((2, rows, 8 * BLK), f32),
            pltpu.VMEM((2, rows, 8 * BLK), jnp.bfloat16),
            pltpu.VMEM((2, rows, 8 * BLK), jnp.bfloat16),
            pltpu.VMEM((2, rows, 1), f32),
            pltpu.SemaphoreType.DMA((2, 8)),
        ],
        compiler_params=pltpu.CompilerParams(vmem_limit_bytes=24 * 2**20),
        cost_estimate=pl.CostEstimate(flops=2**31, bytes_accessed=24 * 2**20, transcendentals=2**21),
        name="attend",
    )(slots, vertical, diag, query, kpv, kpd, *pieces)


def ring(n, step):
    return [(i, (i + step) % n) for i in range(n)]


def after(arrays, dep):
    count = len(arrays)
    hbm = pl.BlockSpec(memory_space=pl.ANY)
    return pl.pallas_call(
        lambda *refs: None,
        out_shape=[jax.ShapeDtypeStruct(a.shape, a.dtype) for a in arrays],
        in_specs=[hbm] * (count + 1),
        out_specs=[hbm] * count,
        input_output_aliases={i: i for i in range(count)},
        name="after",
    )(*arrays, dep)


def up(a):
    return lax.ppermute(a, "tp", ring(lax.axis_size("tp"), 1))


def down(a):
    return lax.ppermute(a, "tp", ring(lax.axis_size("tp"), -1))


def project_kernel(steps, last, place_ref, *refs):
    rows, refs = refs[:8], refs[8:]
    count = len(steps)
    parts = 2 if last else 1
    weights, refs = refs[: count * parts], refs[count * parts :]
    if last:
        before, outs, (wbuf, sems) = refs[0], refs[1:9], refs[9:]
    else:
        acc, wbuf, sems = refs
    n, group, depth = rows[0].shape
    tp = place_ref[0]
    copies = [
        pltpu.make_async_copy(
            w, wbuf.at[i // parts, pl.ds((i % parts) * (depth // parts), depth // parts)], sems.at[i]
        )
        for i, w in enumerate(weights)
    ]
    for c in copies:
        c.start()
    for i, step in enumerate(steps):
        k = lax.rem(tp + step + n, n)
        a = jnp.concatenate([r[k] for r in rows], axis=0)
        for c in copies[i * parts : (i + 1) * parts]:
            c.wait()
        part = jnp.dot(a, wbuf[i], preferred_element_type=jnp.float32)
        if last:
            total = before[...] + part
            for r, out in enumerate(outs):
                out[...] = total[r * group : (r + 1) * group].astype(jnp.bfloat16)
        elif i == 0:
            acc[...] = part
        else:
            acc[...] += part


def project(rows, weights, place, steps, before=None):
    n, group, depth = rows[0].shape
    last = before is not None
    cols = weights[0].shape[1]
    vmem = pl.BlockSpec(memory_space=pltpu.VMEM)
    hbm = pl.BlockSpec(memory_space=pl.ANY)
    if last:
        shapes = [jax.ShapeDtypeStruct((group, cols), jnp.bfloat16)] * 8
    else:
        shapes = jax.ShapeDtypeStruct((8 * group, cols), jnp.float32)
    return pl.pallas_call(
        functools.partial(project_kernel, steps, last),
        out_shape=shapes,
        in_specs=[pl.BlockSpec(memory_space=pltpu.SMEM)]
        + [vmem] * 8
        + [hbm] * len(weights)
        + [vmem] * last,
        out_specs=[vmem] * 8 if last else vmem,
        scratch_shapes=[
            pltpu.VMEM((len(steps), depth, cols), jnp.bfloat16),
            pltpu.SemaphoreType.DMA((len(weights),)),
        ],
        compiler_params=pltpu.CompilerParams(vmem_limit_bytes=32 * 2**20),
        cost_estimate=pl.CostEstimate(
            flops=2**29 * len(steps), bytes_accessed=2**21 * len(steps), transcendentals=0
        ),
        name="project",
    )(place, *rows, *weights, *([before] if last else []))


def per_device(query, keyval, vert_blocks, slash_offsets, counts, out_weight):
    heads, rows, width = query.shape
    seq_index = lax.axis_index("seq")
    tp_index = lax.axis_index("tp")
    core = seq_index % NC
    x_odd = (seq_index // NC) % 2
    y_odd = (seq_index // (NC * NX)) % 2
    block = y_odd * 2 + x_odd
    cols = out_weight.shape[1] // 8
    depth = out_weight.shape[0] // 2
    kv_head = tp_index // (lax.axis_size("tp") // keyval.shape[1])
    own = lax.dynamic_index_in_dim(keyval, kv_head, 1, keepdims=False)
    w0 = lax.dynamic_slice_in_dim(out_weight, (block * 2 + core) * cols, cols, 1)

    near = [own, send(own, A_UP), send(own, A_DOWN), send(own, A_FAR)]
    w_u1, w_d1 = up(w0), down(w0)
    line = jnp.stack(near, axis=1)
    line_k, line_v = (jnp.stack([a[i] for a in near]) for i in range(2))
    up_k, down_v = send(line_k, B_UP), send(line_v, B_DOWN)
    down_k, up_v = send(line_k, B_DOWN), send(line_v, B_UP)
    far_k, far_v = send(up_k, B_UP), send(down_v, B_DOWN)
    w_u1, w_d1 = after([w_u1, w_d1], up_k)
    w_u2, w_d2 = up(w_u1), down(w_d1)
    w_u2, w_d2 = after([w_u2, w_d2], far_v)
    w_u3, w_d3 = up(w_u2), down(w_d2)
    pieces = [line, up_k, down_k, far_k, up_v, down_v, far_v]
    pieces += [send(a, SWAP) for a in pieces]

    def mine(a):
        return lax.dynamic_slice_in_dim(a, tp_index * heads, heads, 0)

    attended = attend(
        query, pieces, shard_slots(seq_index), mine(vert_blocks), mine(slash_offsets),
        mine(counts), seq_index,
    )
    tokens = lax.all_to_all(attended, "tp", split_axis=0, concat_axis=0, tiled=True)
    w_u3, w_d3 = after([w_u3, w_d3], tokens)
    w_u4, w_d4 = up(w_u3[:depth]), down(w_d3[depth:])
    group = [tokens] + [send(tokens, partner(r, 0)) for r in (1, 2, 3)]
    group += [send(a, SWAP) for a in group]
    place = jnp.stack([tp_index, core])
    early = [w0, w_u1, w_d1, w_u2, w_d2, w_u3, w_d3]
    total = project(group, early, place, (0, -1, 1, -2, 2, -3, 3))
    out = project(group, [w_u4, w_d4], place, (4,), total)
    ours = [out[0]] + [send(out[r], partner(r, 0)) for r in (1, 2, 3)]
    theirs = [send(out[r + 4], partner(r, 1)) for r in range(4)]
    first, odd_x, odd_y = core == 0, x_odd == 1, y_odd == 1
    wide = [
        jnp.concatenate([jnp.where(first, a, b), jnp.where(first, b, a)], axis=1)
        for a, b in zip(ours, theirs)
    ]
    wide = [jnp.where(odd_x, wide[i ^ 1], wide[i]) for i in range(4)]
    return jnp.concatenate([jnp.where(odd_y, wide[i ^ 2], wide[i]) for i in range(4)], axis=1)


def solution(mesh):
    return jax.shard_map(
        per_device,
        mesh=mesh,
        in_specs=(P("tp", "seq", None), P(None, None, "seq", None), P(), P(), P(), P("tp", None)),
        out_specs=P(("seq", "tp"), None),
        check_vma=False,
    )
```

```python
import functools
import math

import jax
import jax.numpy as jnp
from jax import lax
from jax.experimental import pallas as pl
from jax.experimental.pallas import tpu as pltpu
from jax.sharding import PartitionSpec as P

BLK = 64
NY, NX, NC = 4, 4, 2
DEAD = 1 << 20
SCALE = math.log2(math.e)


def seq_perm(move):
    pairs = []
    for y in range(NY):
        for x in range(NX):
            for c in range(NC):
                ty, tx, tc = move(y, x, c)
                pairs.append(((y * NX + x) * NC + c, ((ty % NY) * NX + tx % NX) * NC + tc))
    return pairs


A_UP = seq_perm(lambda y, x, c: (y, x + 1, c) if c == 0 else (y + 1, x, c))
A_DOWN = seq_perm(lambda y, x, c: (y, x - 1, c) if c == 0 else (y - 1, x, c))
A_FAR = seq_perm(lambda y, x, c: (y, x + 2, c) if c == 0 else (y + 2, x, c))
B_UP = seq_perm(lambda y, x, c: (y + 1, x, c) if c == 0 else (y, x + 1, c))
B_DOWN = seq_perm(lambda y, x, c: (y - 1, x, c) if c == 0 else (y, x - 1, c))
def pair(v, c):
    return (v ^ 1) if c == 0 else (v + 1 if v % 2 else v - 1)


def partner(r, other):
    return seq_perm(
        lambda y, x, c: (
            pair(y, c ^ other) if r & 2 else y,
            pair(x, c ^ other) if r & 1 else x,
            c ^ other,
        )
    )


SWAP = seq_perm(lambda y, x, c: (y, x, 1 - c))


def send(a, pairs):
    return lax.ppermute(a, "seq", pairs)


def shard_slots(seq_index):
    shard = jnp.arange(NY * NX * NC, dtype=jnp.int32)

    def parts(i):
        return i // (NX * NC), (i // NC) % NX, i % NC

    ys, xs, cs = parts(shard)
    y0, x0, c0 = parts(seq_index)
    order = jnp.array([0, 2, 3, 1], jnp.int32)
    in_y, in_x = order[(ys - y0) % NY], order[(xs - x0) % NX]
    first = jnp.where(cs == 0, in_x, in_y)
    second = jnp.where(cs == 0, in_y, in_x)
    return (cs != c0) * 16 + second * 4 + first


def attend_kernel(slots_ref, vert_ref, diag_ref, q_ref, kpv_ref, kpd_ref, *refs):
    pieces, o_ref = refs[:16], refs[16]
    kbuf, vbuf, sv_ref, sd_ref, pv_ref, pd_ref, tot_ref, sems = refs[17:]
    heads, rows, width = q_ref.shape
    blocks = rows // BLK
    per = rows // BLK
    copies = ([], [])
    for side in range(2):
        for which, buf in enumerate((kbuf, vbuf)):
            for j in range(4):
                src = pieces[side * 8 + which * 4 + j]
                copies[which].append(
                    pltpu.make_async_copy(
                        src, buf.at[pl.ds(side * 16 + j * 4, 4)], sems.at[which, side * 4 + j]
                    )
                )
    for c in copies[0] + copies[1]:
        c.start()
    for c in copies[0]:
        c.wait()

    def tile(buf, block):
        return buf[slots_ref[block // per], pl.ds(pl.multiple_of((block % per) * BLK, BLK), BLK), :]

    scale = SCALE / math.sqrt(width)
    nt = (((1,), (1,)), ((), ()))

    def one_head(h):
        verts = [vert_ref[h, c] for c in range(8)]
        diags = [[diag_ref[h * blocks + b, c] for c in range(8)] for b in range(blocks)]
        sv, sd, pv, pd, tot = (r.at[h % 2] for r in (sv_ref, sd_ref, pv_ref, pd_ref, tot_ref))
        k_v = jnp.concatenate([tile(kbuf, v) for v in verts], axis=0)
        sv[...] = lax.dot_general(q_ref[h], k_v, nt, preferred_element_type=jnp.float32)
        for b in range(blocks):
            r = slice(b * BLK, (b + 1) * BLK)
            k_d = jnp.concatenate([tile(kbuf, v) for v in diags[b]], axis=0)
            sd[r, :] = lax.dot_general(q_ref[h, r, :], k_d, nt, preferred_element_type=jnp.float32)
        kpv = kpv_ref[h]
        for b in range(blocks):
            r = slice(b * BLK, (b + 1) * BLK)
            qpos = b * BLK + lax.broadcasted_iota(jnp.int32, (BLK, 1), 0)
            s_d = jnp.where(kpd_ref[h * blocks + b] <= qpos, sd[r, :], -1e30)
            s_v = jnp.where(kpv <= qpos, sv[r, :], -1e30)
            top = jnp.maximum(
                jnp.max(s_d, axis=1, keepdims=True), jnp.max(s_v, axis=1, keepdims=True)
            )
            p_d = jnp.exp2((s_d - top) * scale)
            p_v = jnp.exp2((s_v - top) * scale)
            tot[r, :] = jnp.sum(p_d, axis=1, keepdims=True) + jnp.sum(p_v, axis=1, keepdims=True)
            pv[r, :] = p_v.astype(jnp.bfloat16)
            pd[r, :] = p_d.astype(jnp.bfloat16)
        if h == 0:
            for c in copies[1]:
                c.wait()
        v_v = jnp.concatenate([tile(vbuf, v) for v in verts], axis=0)
        o_v = jnp.dot(pv[...], v_v, preferred_element_type=jnp.float32)
        for b in range(blocks):
            r = slice(b * BLK, (b + 1) * BLK)
            v_d = jnp.concatenate([tile(vbuf, v) for v in diags[b]], axis=0)
            o_d = jnp.dot(pd[r, :], v_d, preferred_element_type=jnp.float32)
            o = ((o_v[r] + o_d) / tot[r, :]).astype(jnp.bfloat16)
            o_ref[b, :, h * width : (h + 1) * width] = o

    for h in range(heads):
        one_head(h)


def attend(query, pieces, slots, vertical, slash, counts, seq_index):
    heads, rows, width = query.shape
    blocks = rows // BLK
    slot = jnp.arange(8, dtype=jnp.int32)
    first = seq_index * blocks
    vert_live = slot[None, :] < counts[:, 0:1]
    diag = first + jnp.arange(blocks, dtype=jnp.int32)[None, :, None] - slash[:, None, :]
    covered = jnp.any(
        (diag[:, :, :, None] == vertical[:, None, None, :]) & vert_live[:, None, None, :], axis=3
    )
    diag_live = (slot < counts[:, 1:2])[:, None, :] & (diag >= 0) & jnp.logical_not(covered)
    within = jnp.arange(BLK, dtype=jnp.int32)
    kpv = jnp.where(
        vert_live[:, :, None], (vertical - first)[:, :, None] * BLK + within, DEAD
    ).reshape(heads, 1, 8 * BLK)
    kpd = jnp.where(
        diag_live[:, :, :, None], (diag - first)[:, :, :, None] * BLK + within, DEAD
    ).reshape(heads * blocks, 1, 8 * BLK)
    diag = jnp.maximum(diag, 0).reshape(heads * blocks, 8)
    smem = pl.BlockSpec(memory_space=pltpu.SMEM)
    vmem = pl.BlockSpec(memory_space=pltpu.VMEM)
    hbm = pl.BlockSpec(memory_space=pl.ANY)
    f32 = jnp.float32
    return pl.pallas_call(
        attend_kernel,
        out_shape=jax.ShapeDtypeStruct((blocks, BLK, heads * width), jnp.bfloat16),
        in_specs=[smem] * 3 + [vmem] * 3 + [hbm] * len(pieces),
        out_specs=vmem,
        scratch_shapes=[
            pltpu.VMEM((32, rows, width), jnp.bfloat16),
            pltpu.VMEM((32, rows, width), jnp.bfloat16),
            pltpu.VMEM((2, rows, 8 * BLK), f32),
            pltpu.VMEM((2, rows, 8 * BLK), f32),
            pltpu.VMEM((2, rows, 8 * BLK), jnp.bfloat16),
            pltpu.VMEM((2, rows, 8 * BLK), jnp.bfloat16),
            pltpu.VMEM((2, rows, 1), f32),
            pltpu.SemaphoreType.DMA((2, 8)),
        ],
        compiler_params=pltpu.CompilerParams(vmem_limit_bytes=24 * 2**20),
        cost_estimate=pl.CostEstimate(flops=2**31, bytes_accessed=24 * 2**20, transcendentals=2**21),
        name="attend",
    )(slots, vertical, diag, query, kpv, kpd, *pieces)


def ring(n, step):
    return [(i, (i + step) % n) for i in range(n)]


def after(arrays, dep):
    count = len(arrays)
    hbm = pl.BlockSpec(memory_space=pl.ANY)
    return pl.pallas_call(
        lambda *refs: None,
        out_shape=[jax.ShapeDtypeStruct(a.shape, a.dtype) for a in arrays],
        in_specs=[hbm] * (count + 1),
        out_specs=[hbm] * count,
        input_output_aliases={i: i for i in range(count)},
        name="after",
    )(*arrays, dep)


def up(a):
    return lax.ppermute(a, "tp", ring(lax.axis_size("tp"), 1))


def down(a):
    return lax.ppermute(a, "tp", ring(lax.axis_size("tp"), -1))


def project_kernel(steps, last, place_ref, *refs):
    rows, refs = refs[:8], refs[8:]
    count = len(steps)
    parts = 2 if last else 1
    weights, refs = refs[: count * parts], refs[count * parts :]
    if last:
        before, outs, (wbuf, sems) = refs[0], refs[1:9], refs[9:]
    else:
        acc, wbuf, sems = refs
    n, group, depth = rows[0].shape
    tp = place_ref[0]
    copies = [
        pltpu.make_async_copy(
            w, wbuf.at[i // parts, pl.ds((i % parts) * (depth // parts), depth // parts)], sems.at[i]
        )
        for i, w in enumerate(weights)
    ]
    for c in copies:
        c.start()
    for i, step in enumerate(steps):
        k = lax.rem(tp + step + n, n)
        a = jnp.concatenate([r[k] for r in rows], axis=0)
        for c in copies[i * parts : (i + 1) * parts]:
            c.wait()
        part = jnp.dot(a, wbuf[i], preferred_element_type=jnp.float32)
        if last:
            total = before[...] + part
            for r, out in enumerate(outs):
                out[...] = total[r * group : (r + 1) * group].astype(jnp.bfloat16)
        elif i == 0:
            acc[...] = part
        else:
            acc[...] += part


def project(rows, weights, place, steps, before=None):
    n, group, depth = rows[0].shape
    last = before is not None
    cols = weights[0].shape[1]
    vmem = pl.BlockSpec(memory_space=pltpu.VMEM)
    hbm = pl.BlockSpec(memory_space=pltpu.HBM)
    if last:
        shapes = [jax.ShapeDtypeStruct((group, cols), jnp.bfloat16)] * 8
    else:
        shapes = jax.ShapeDtypeStruct((8 * group, cols), jnp.float32)
    return pl.pallas_call(
        functools.partial(project_kernel, steps, last),
        out_shape=shapes,
        in_specs=[pl.BlockSpec(memory_space=pltpu.SMEM)]
        + [vmem] * 8
        + [hbm] * len(weights)
        + [vmem] * last,
        out_specs=[vmem] * 8 if last else vmem,
        scratch_shapes=[
            pltpu.VMEM((len(steps), depth, cols), jnp.bfloat16),
            pltpu.SemaphoreType.DMA((len(weights),)),
        ],
        compiler_params=pltpu.CompilerParams(vmem_limit_bytes=32 * 2**20),
        cost_estimate=pl.CostEstimate(
            flops=2**29 * len(steps), bytes_accessed=2**21 * len(steps), transcendentals=0
        ),
        name="project",
    )(place, *rows, *weights, *([before] if last else []))


def per_device(query, keyval, vert_blocks, slash_offsets, counts, out_weight):
    heads, rows, width = query.shape
    seq_index = lax.axis_index("seq")
    tp_index = lax.axis_index("tp")
    core = seq_index % NC
    x_odd = (seq_index // NC) % 2
    y_odd = (seq_index // (NC * NX)) % 2
    block = y_odd * 2 + x_odd
    cols = out_weight.shape[1] // 8
    depth = out_weight.shape[0] // 2
    kv_head = tp_index // (lax.axis_size("tp") // keyval.shape[1])
    own = lax.dynamic_index_in_dim(keyval, kv_head, 1, keepdims=False)
    w0 = lax.dynamic_slice_in_dim(out_weight, (block * 2 + core) * cols, cols, 1)
    near = [own, send(own, A_UP), send(own, A_DOWN), send(own, A_FAR)]
    w_u1, w_d1 = up(w0), down(w0)
    line_k, line_v = (jnp.stack([a[i] for a in near]) for i in range(2))
    up_k, down_v = send(line_k, B_UP), send(line_v, B_DOWN)
    down_k, up_v = send(line_k, B_DOWN), send(line_v, B_UP)
    far_k, far_v = send(up_k, B_UP), send(down_v, B_DOWN)
    pieces = [line_k, up_k, down_k, far_k, line_v, up_v, down_v, far_v]
    pieces += [send(a, SWAP) for a in pieces]
    w_u1, w_d1 = after([w_u1, w_d1], up_k)
    w_u2, w_d2 = up(w_u1), down(w_d1)

    def mine(a):
        return lax.dynamic_slice_in_dim(a, tp_index * heads, heads, 0)

    attended = attend(
        query, pieces, shard_slots(seq_index), mine(vert_blocks), mine(slash_offsets),
        mine(counts), seq_index,
    )
    w_u2, w_d2 = after([w_u2, w_d2], attended)
    w_u3, w_d3 = up(w_u2), down(w_d2)
    tokens = lax.all_to_all(attended, "tp", split_axis=0, concat_axis=0, tiled=True)
    w_u3, w_d3 = after([w_u3, w_d3], tokens)
    w_u4, w_d4 = up(w_u3[:depth]), down(w_d3[depth:])
    group = [tokens] + [send(tokens, partner(r, 0)) for r in (1, 2, 3)]
    group += [send(a, SWAP) for a in group]
    place = jnp.stack([tp_index, core])
    early = [w0, w_u1, w_d1, w_u2, w_d2, w_u3, w_d3]
    total = project(group, early, place, (0, -1, 1, -2, 2, -3, 3))
    out = project(group, [w_u4, w_d4], place, (4,), total)
    ours = [out[0]] + [send(out[r], partner(r, 0)) for r in (1, 2, 3)]
    theirs = [send(out[r + 4], partner(r, 1)) for r in range(4)]
    first, odd_x, odd_y = core == 0, x_odd == 1, y_odd == 1
    wide = [
        jnp.concatenate([jnp.where(first, a, b), jnp.where(first, b, a)], axis=1)
        for a, b in zip(ours, theirs)
    ]
    wide = [jnp.where(odd_x, wide[i ^ 1], wide[i]) for i in range(4)]
    return jnp.concatenate([jnp.where(odd_y, wide[i ^ 2], wide[i]) for i in range(4)], axis=1)


def solution(mesh):
    return jax.shard_map(
        per_device,
        mesh=mesh,
        in_specs=(P("tp", "seq", None), P(None, None, "seq", None), P(), P(), P(), P("tp", None)),
        out_specs=P(("seq", "tp"), None),
        check_vma=False,
    )
```

```python
import functools
import math

import jax
import jax.numpy as jnp
from jax import lax
from jax.experimental import pallas as pl
from jax.experimental.pallas import tpu as pltpu
from jax.sharding import PartitionSpec as P

BLK = 64
NY, NX, NC = 4, 4, 2
DEAD = 1 << 20
SCALE = math.log2(math.e)


def seq_perm(move):
    pairs = []
    for y in range(NY):
        for x in range(NX):
            for c in range(NC):
                ty, tx, tc = move(y, x, c)
                pairs.append(((y * NX + x) * NC + c, ((ty % NY) * NX + tx % NX) * NC + tc))
    return pairs


A_UP = seq_perm(lambda y, x, c: (y, x + 1, c) if c == 0 else (y + 1, x, c))
A_DOWN = seq_perm(lambda y, x, c: (y, x - 1, c) if c == 0 else (y - 1, x, c))
A_FAR = seq_perm(lambda y, x, c: (y, x + 2, c) if c == 0 else (y + 2, x, c))
B_UP = seq_perm(lambda y, x, c: (y + 1, x, c) if c == 0 else (y, x + 1, c))
B_DOWN = seq_perm(lambda y, x, c: (y - 1, x, c) if c == 0 else (y, x - 1, c))
def pair(v, c):
    return (v ^ 1) if c == 0 else (v + 1 if v % 2 else v - 1)


def partner(r, other):
    return seq_perm(
        lambda y, x, c: (
            pair(y, c ^ other) if r & 2 else y,
            pair(x, c ^ other) if r & 1 else x,
            c ^ other,
        )
    )


SWAP = seq_perm(lambda y, x, c: (y, x, 1 - c))


def send(a, pairs):
    return lax.ppermute(a, "seq", pairs)


def shard_slots(seq_index):
    shard = jnp.arange(NY * NX * NC, dtype=jnp.int32)

    def parts(i):
        return i // (NX * NC), (i // NC) % NX, i % NC

    ys, xs, cs = parts(shard)
    y0, x0, c0 = parts(seq_index)
    order = jnp.array([0, 2, 3, 1], jnp.int32)
    in_y, in_x = order[(ys - y0) % NY], order[(xs - x0) % NX]
    first = jnp.where(cs == 0, in_x, in_y)
    second = jnp.where(cs == 0, in_y, in_x)
    return (cs != c0) * 16 + second * 4 + first


def attend_kernel(slots_ref, vert_ref, diag_ref, q_ref, kpv_ref, kpd_ref, *refs):
    pieces, o_ref = refs[:16], refs[16]
    kbuf, vbuf, sv_ref, sd_ref, pv_ref, pd_ref, tot_ref, sems = refs[17:]
    heads, rows, width = q_ref.shape
    blocks = rows // BLK
    per = rows // BLK
    copies = ([], [])
    for side in range(2):
        for which, buf in enumerate((kbuf, vbuf)):
            for j in range(4):
                src = pieces[side * 8 + which * 4 + j]
                copies[which].append(
                    pltpu.make_async_copy(
                        src, buf.at[pl.ds(side * 16 + j * 4, 4)], sems.at[which, side * 4 + j]
                    )
                )
    for c in copies[0] + copies[1]:
        c.start()
    for c in copies[0]:
        c.wait()

    def tile(buf, block):
        return buf[slots_ref[block // per], pl.ds(pl.multiple_of((block % per) * BLK, BLK), BLK), :]

    scale = SCALE / math.sqrt(width)
    nt = (((1,), (1,)), ((), ()))

    def one_head(h, carry):
        verts = [vert_ref[h, c] for c in range(8)]
        diags = [[diag_ref[h * blocks + b, c] for c in range(8)] for b in range(blocks)]
        sv, sd, pv, pd, tot = (r.at[h % 2] for r in (sv_ref, sd_ref, pv_ref, pd_ref, tot_ref))
        k_v = jnp.concatenate([tile(kbuf, v) for v in verts], axis=0)
        sv[...] = lax.dot_general(q_ref[h], k_v, nt, preferred_element_type=jnp.float32)
        for b in range(blocks):
            r = slice(b * BLK, (b + 1) * BLK)
            k_d = jnp.concatenate([tile(kbuf, v) for v in diags[b]], axis=0)
            sd[r, :] = lax.dot_general(q_ref[h, r, :], k_d, nt, preferred_element_type=jnp.float32)
        kpv = kpv_ref[h]
        for b in range(blocks):
            r = slice(b * BLK, (b + 1) * BLK)
            qpos = b * BLK + lax.broadcasted_iota(jnp.int32, (BLK, 1), 0)
            s_d = jnp.where(kpd_ref[h * blocks + b] <= qpos, sd[r, :], -1e30)
            s_v = jnp.where(kpv <= qpos, sv[r, :], -1e30)
            top = jnp.maximum(
                jnp.max(s_d, axis=1, keepdims=True), jnp.max(s_v, axis=1, keepdims=True)
            )
            p_d = jnp.exp2((s_d - top) * scale)
            p_v = jnp.exp2((s_v - top) * scale)
            tot[r, :] = jnp.sum(p_d, axis=1, keepdims=True) + jnp.sum(p_v, axis=1, keepdims=True)
            pv[r, :] = p_v.astype(jnp.bfloat16)
            pd[r, :] = p_d.astype(jnp.bfloat16)

        @pl.when(h == 0)
        def _():
            for c in copies[1]:
                c.wait()

        v_v = jnp.concatenate([tile(vbuf, v) for v in verts], axis=0)
        o_v = jnp.dot(pv[...], v_v, preferred_element_type=jnp.float32)
        for b in range(blocks):
            r = slice(b * BLK, (b + 1) * BLK)
            v_d = jnp.concatenate([tile(vbuf, v) for v in diags[b]], axis=0)
            o_d = jnp.dot(pd[r, :], v_d, preferred_element_type=jnp.float32)
            o = ((o_v[r] + o_d) / tot[r, :]).astype(jnp.bfloat16)
            o_ref[b, :, pl.ds(pl.multiple_of(h * width, width), width)] = o
        return carry

    lax.fori_loop(0, heads, one_head, 0)


def attend(query, pieces, slots, vertical, slash, counts, seq_index):
    heads, rows, width = query.shape
    blocks = rows // BLK
    slot = jnp.arange(8, dtype=jnp.int32)
    first = seq_index * blocks
    vert_live = slot[None, :] < counts[:, 0:1]
    diag = first + jnp.arange(blocks, dtype=jnp.int32)[None, :, None] - slash[:, None, :]
    covered = jnp.any(
        (diag[:, :, :, None] == vertical[:, None, None, :]) & vert_live[:, None, None, :], axis=3
    )
    diag_live = (slot < counts[:, 1:2])[:, None, :] & (diag >= 0) & jnp.logical_not(covered)
    within = jnp.arange(BLK, dtype=jnp.int32)
    kpv = jnp.where(
        vert_live[:, :, None], (vertical - first)[:, :, None] * BLK + within, DEAD
    ).reshape(heads, 1, 8 * BLK)
    kpd = jnp.where(
        diag_live[:, :, :, None], (diag - first)[:, :, :, None] * BLK + within, DEAD
    ).reshape(heads * blocks, 1, 8 * BLK)
    diag = jnp.maximum(diag, 0).reshape(heads * blocks, 8)
    smem = pl.BlockSpec(memory_space=pltpu.SMEM)
    vmem = pl.BlockSpec(memory_space=pltpu.VMEM)
    hbm = pl.BlockSpec(memory_space=pl.ANY)
    f32 = jnp.float32
    return pl.pallas_call(
        attend_kernel,
        out_shape=jax.ShapeDtypeStruct((blocks, BLK, heads * width), jnp.bfloat16),
        in_specs=[smem] * 3 + [vmem] * 3 + [hbm] * len(pieces),
        out_specs=vmem,
        scratch_shapes=[
            pltpu.VMEM((32, rows, width), jnp.bfloat16),
            pltpu.VMEM((32, rows, width), jnp.bfloat16),
            pltpu.VMEM((2, rows, 8 * BLK), f32),
            pltpu.VMEM((2, rows, 8 * BLK), f32),
            pltpu.VMEM((2, rows, 8 * BLK), jnp.bfloat16),
            pltpu.VMEM((2, rows, 8 * BLK), jnp.bfloat16),
            pltpu.VMEM((2, rows, 1), f32),
            pltpu.SemaphoreType.DMA((2, 8)),
        ],
        compiler_params=pltpu.CompilerParams(vmem_limit_bytes=24 * 2**20),
        cost_estimate=pl.CostEstimate(flops=2**31, bytes_accessed=24 * 2**20, transcendentals=2**21),
        name="attend",
    )(slots, vertical, diag, query, kpv, kpd, *pieces)


def ring(n, step):
    return [(i, (i + step) % n) for i in range(n)]


def after(arrays, dep):
    count = len(arrays)
    hbm = pl.BlockSpec(memory_space=pl.ANY)
    return pl.pallas_call(
        lambda *refs: None,
        out_shape=[jax.ShapeDtypeStruct(a.shape, a.dtype) for a in arrays],
        in_specs=[hbm] * (count + 1),
        out_specs=[hbm] * count,
        input_output_aliases={i: i for i in range(count)},
        name="after",
    )(*arrays, dep)


def up(a):
    return lax.ppermute(a, "tp", ring(lax.axis_size("tp"), 1))


def down(a):
    return lax.ppermute(a, "tp", ring(lax.axis_size("tp"), -1))


def project_kernel(steps, last, place_ref, *refs):
    rows, refs = refs[:8], refs[8:]
    count = len(steps)
    parts = 2 if last else 1
    weights, refs = refs[: count * parts], refs[count * parts :]
    if last:
        before, outs, (wbuf, sems) = refs[0], refs[1:9], refs[9:]
    else:
        acc, wbuf, sems = refs
    n, group, depth = rows[0].shape
    tp = place_ref[0]
    copies = [
        pltpu.make_async_copy(
            w, wbuf.at[i // parts, pl.ds((i % parts) * (depth // parts), depth // parts)], sems.at[i]
        )
        for i, w in enumerate(weights)
    ]
    for c in copies:
        c.start()
    def product(i, hops):
        k = lax.rem(tp + hops + n, n)
        a = jnp.concatenate([r[k] for r in rows], axis=0)
        return jnp.dot(a, wbuf[i], preferred_element_type=jnp.float32)

    if last:
        for c in copies:
            c.wait()
        total = before[...] + product(0, steps[0])
        for r, out in enumerate(outs):
            out[...] = total[r * group : (r + 1) * group].astype(jnp.bfloat16)
    else:
        copies[0].wait()
        acc[...] = product(0, 0)

        def add(i, carry):
            pltpu.make_async_copy(wbuf.at[i], wbuf.at[i], sems.at[i]).wait()
            hops = (i + 1) // 2
            acc[...] += product(i, jnp.where(i % 2 == 1, -hops, hops))
            return carry

        lax.fori_loop(1, count, add, 0)


def project(rows, weights, place, steps, before=None):
    n, group, depth = rows[0].shape
    last = before is not None
    cols = weights[0].shape[1]
    vmem = pl.BlockSpec(memory_space=pltpu.VMEM)
    hbm = pl.BlockSpec(memory_space=pltpu.HBM)
    if last:
        shapes = [jax.ShapeDtypeStruct((group, cols), jnp.bfloat16)] * 8
    else:
        shapes = jax.ShapeDtypeStruct((8 * group, cols), jnp.float32)
    return pl.pallas_call(
        functools.partial(project_kernel, steps, last),
        out_shape=shapes,
        in_specs=[pl.BlockSpec(memory_space=pltpu.SMEM)]
        + [vmem] * 8
        + [hbm] * len(weights)
        + [vmem] * last,
        out_specs=[vmem] * 8 if last else vmem,
        scratch_shapes=[
            pltpu.VMEM((len(steps), depth, cols), jnp.bfloat16),
            pltpu.SemaphoreType.DMA((len(weights),)),
        ],
        compiler_params=pltpu.CompilerParams(vmem_limit_bytes=32 * 2**20),
        cost_estimate=pl.CostEstimate(
            flops=2**29 * len(steps), bytes_accessed=2**21 * len(steps), transcendentals=0
        ),
        name="project",
    )(place, *rows, *weights, *([before] if last else []))


def per_device(query, keyval, vert_blocks, slash_offsets, counts, out_weight):
    heads, rows, width = query.shape
    seq_index = lax.axis_index("seq")
    tp_index = lax.axis_index("tp")
    core = seq_index % NC
    x_odd = (seq_index // NC) % 2
    y_odd = (seq_index // (NC * NX)) % 2
    block = y_odd * 2 + x_odd
    cols = out_weight.shape[1] // 8
    depth = out_weight.shape[0] // 2
    kv_head = tp_index // (lax.axis_size("tp") // keyval.shape[1])
    own = lax.dynamic_index_in_dim(keyval, kv_head, 1, keepdims=False)
    w0 = lax.dynamic_slice_in_dim(out_weight, (block * 2 + core) * cols, cols, 1)
    near = [own, send(own, A_UP), send(own, A_DOWN), send(own, A_FAR)]
    w_u1, w_d1 = up(w0), down(w0)
    line_k, line_v = (jnp.stack([a[i] for a in near]) for i in range(2))
    up_k, down_v = send(line_k, B_UP), send(line_v, B_DOWN)
    down_k, up_v = send(line_k, B_DOWN), send(line_v, B_UP)
    far_k, far_v = send(up_k, B_UP), send(down_v, B_DOWN)
    pieces = [line_k, up_k, down_k, far_k, line_v, up_v, down_v, far_v]
    pieces += [send(a, SWAP) for a in pieces]
    w_u1, w_d1 = after([w_u1, w_d1], up_k)
    w_u2, w_d2 = up(w_u1), down(w_d1)

    def mine(a):
        return lax.dynamic_slice_in_dim(a, tp_index * heads, heads, 0)

    attended = attend(
        query, pieces, shard_slots(seq_index), mine(vert_blocks), mine(slash_offsets),
        mine(counts), seq_index,
    )
    w_u2, w_d2 = after([w_u2, w_d2], attended)
    w_u3, w_d3 = up(w_u2), down(w_d2)
    tokens = lax.all_to_all(attended, "tp", split_axis=0, concat_axis=0, tiled=True)
    w_u3, w_d3 = after([w_u3, w_d3], tokens)
    w_u4, w_d4 = up(w_u3[:depth]), down(w_d3[depth:])
    group = [tokens] + [send(tokens, partner(r, 0)) for r in (1, 2, 3)]
    group += [send(a, SWAP) for a in group]
    place = jnp.stack([tp_index, core])
    early = [w0, w_u1, w_d1, w_u2, w_d2, w_u3, w_d3]
    total = project(group, early, place, (0, -1, 1, -2, 2, -3, 3))
    out = project(group, [w_u4, w_d4], place, (4,), total)
    ours = [out[0]] + [send(out[r], partner(r, 0)) for r in (1, 2, 3)]
    theirs = [send(out[r + 4], partner(r, 1)) for r in range(4)]
    first, odd_x, odd_y = core == 0, x_odd == 1, y_odd == 1
    wide = [
        jnp.concatenate([jnp.where(first, a, b), jnp.where(first, b, a)], axis=1)
        for a, b in zip(ours, theirs)
    ]
    wide = [jnp.where(odd_x, wide[i ^ 1], wide[i]) for i in range(4)]
    return jnp.concatenate([jnp.where(odd_y, wide[i ^ 2], wide[i]) for i in range(4)], axis=1)


def solution(mesh):
    return jax.shard_map(
        per_device,
        mesh=mesh,
        in_specs=(P("tp", "seq", None), P(None, None, "seq", None), P(), P(), P(), P("tp", None)),
        out_specs=P(("seq", "tp"), None),
        check_vma=False,
    )
```

```python
import functools
import math

import jax
import jax.numpy as jnp
from jax import lax
from jax.experimental import pallas as pl
from jax.experimental.pallas import tpu as pltpu
from jax.sharding import PartitionSpec as P

BLK = 64
NY, NX, NC = 4, 4, 2
DEAD = 1 << 20
SCALE = math.log2(math.e)


def seq_perm(move):
    pairs = []
    for y in range(NY):
        for x in range(NX):
            for c in range(NC):
                ty, tx, tc = move(y, x, c)
                pairs.append(((y * NX + x) * NC + c, ((ty % NY) * NX + tx % NX) * NC + tc))
    return pairs


A_UP = seq_perm(lambda y, x, c: (y, x + 1, c) if c == 0 else (y + 1, x, c))
A_DOWN = seq_perm(lambda y, x, c: (y, x - 1, c) if c == 0 else (y - 1, x, c))
A_FAR = seq_perm(lambda y, x, c: (y, x + 2, c) if c == 0 else (y + 2, x, c))
B_UP = seq_perm(lambda y, x, c: (y + 1, x, c) if c == 0 else (y, x + 1, c))
B_DOWN = seq_perm(lambda y, x, c: (y - 1, x, c) if c == 0 else (y, x - 1, c))
def pair(v, c):
    return (v ^ 1) if c == 0 else (v + 1 if v % 2 else v - 1)


def partner(r, other):
    return seq_perm(
        lambda y, x, c: (
            pair(y, c ^ other) if r & 2 else y,
            pair(x, c ^ other) if r & 1 else x,
            c ^ other,
        )
    )


SWAP = seq_perm(lambda y, x, c: (y, x, 1 - c))


def send(a, pairs):
    return lax.ppermute(a, "seq", pairs)


def shard_slots(seq_index):
    shard = jnp.arange(NY * NX * NC, dtype=jnp.int32)

    def parts(i):
        return i // (NX * NC), (i // NC) % NX, i % NC

    ys, xs, cs = parts(shard)
    y0, x0, c0 = parts(seq_index)
    order = jnp.array([0, 2, 3, 1], jnp.int32)
    in_y, in_x = order[(ys - y0) % NY], order[(xs - x0) % NX]
    first = jnp.where(cs == 0, in_x, in_y)
    second = jnp.where(cs == 0, in_y, in_x)
    return (cs != c0) * 16 + second * 4 + first


def attend_kernel(slots_ref, vert_ref, diag_ref, q_ref, kpv_ref, kpd_ref, *refs):
    pieces, o_ref = refs[:16], refs[16]
    kbuf, vbuf, sv_ref, sd_ref, pv_ref, pd_ref, tot_ref, sems = refs[17:]
    heads, rows, width = q_ref.shape
    blocks = rows // BLK
    per = rows // BLK
    copies = ([], [])
    for side in range(2):
        for which, buf in enumerate((kbuf, vbuf)):
            for j in range(4):
                src = pieces[side * 8 + which * 4 + j]
                copies[which].append(
                    pltpu.make_async_copy(
                        src, buf.at[pl.ds(side * 16 + j * 4, 4)], sems.at[which, side * 4 + j]
                    )
                )
    for c in copies[0] + copies[1]:
        c.start()
    for c in copies[0]:
        c.wait()

    def tile(buf, block):
        return buf[slots_ref[block // per], pl.ds(pl.multiple_of((block % per) * BLK, BLK), BLK), :]

    scale = SCALE / math.sqrt(width)
    nt = (((1,), (1,)), ((), ()))

    def one_head(h, carry):
        verts = [vert_ref[h, c] for c in range(8)]
        diags = [[diag_ref[h * blocks + b, c] for c in range(8)] for b in range(blocks)]
        sv, sd, pv, pd, tot = (r.at[h % 2] for r in (sv_ref, sd_ref, pv_ref, pd_ref, tot_ref))
        k_v = jnp.concatenate([tile(kbuf, v) for v in verts], axis=0)
        sv[...] = lax.dot_general(q_ref[h], k_v, nt, preferred_element_type=jnp.float32)
        for b in range(blocks):
            r = slice(b * BLK, (b + 1) * BLK)
            k_d = jnp.concatenate([tile(kbuf, v) for v in diags[b]], axis=0)
            sd[r, :] = lax.dot_general(q_ref[h, r, :], k_d, nt, preferred_element_type=jnp.float32)
        kpv = kpv_ref[h]
        for b in range(blocks):
            r = slice(b * BLK, (b + 1) * BLK)
            qpos = b * BLK + lax.broadcasted_iota(jnp.int32, (BLK, 1), 0)
            s_d = jnp.where(kpd_ref[h * blocks + b] <= qpos, sd[r, :], -1e30)
            s_v = jnp.where(kpv <= qpos, sv[r, :], -1e30)
            top = jnp.maximum(
                jnp.max(s_d, axis=1, keepdims=True), jnp.max(s_v, axis=1, keepdims=True)
            )
            p_d = jnp.exp2((s_d - top) * scale)
            p_v = jnp.exp2((s_v - top) * scale)
            tot[r, :] = jnp.sum(p_d, axis=1, keepdims=True) + jnp.sum(p_v, axis=1, keepdims=True)
            pv[r, :] = p_v.astype(jnp.bfloat16)
            pd[r, :] = p_d.astype(jnp.bfloat16)

        @pl.when(h == 0)
        def _():
            for c in copies[1]:
                c.wait()

        v_v = jnp.concatenate([tile(vbuf, v) for v in verts], axis=0)
        o_v = jnp.dot(pv[...], v_v, preferred_element_type=jnp.float32)
        for b in range(blocks):
            r = slice(b * BLK, (b + 1) * BLK)
            v_d = jnp.concatenate([tile(vbuf, v) for v in diags[b]], axis=0)
            o_d = jnp.dot(pd[r, :], v_d, preferred_element_type=jnp.float32)
            o = ((o_v[r] + o_d) / tot[r, :]).astype(jnp.bfloat16)
            o_ref[b, :, pl.ds(pl.multiple_of(h * width, width), width)] = o
        return carry

    lax.fori_loop(0, heads, one_head, 0)


def attend(query, pieces, slots, vertical, slash, counts, seq_index):
    heads, rows, width = query.shape
    blocks = rows // BLK
    slot = jnp.arange(8, dtype=jnp.int32)
    first = seq_index * blocks
    vert_live = slot[None, :] < counts[:, 0:1]
    diag = first + jnp.arange(blocks, dtype=jnp.int32)[None, :, None] - slash[:, None, :]
    covered = jnp.any(
        (diag[:, :, :, None] == vertical[:, None, None, :]) & vert_live[:, None, None, :], axis=3
    )
    diag_live = (slot < counts[:, 1:2])[:, None, :] & (diag >= 0) & jnp.logical_not(covered)
    within = jnp.arange(BLK, dtype=jnp.int32)
    kpv = jnp.where(
        vert_live[:, :, None], (vertical - first)[:, :, None] * BLK + within, DEAD
    ).reshape(heads, 1, 8 * BLK)
    kpd = jnp.where(
        diag_live[:, :, :, None], (diag - first)[:, :, :, None] * BLK + within, DEAD
    ).reshape(heads * blocks, 1, 8 * BLK)
    diag = jnp.maximum(diag, 0).reshape(heads * blocks, 8)
    smem = pl.BlockSpec(memory_space=pltpu.SMEM)
    vmem = pl.BlockSpec(memory_space=pltpu.VMEM)
    hbm = pl.BlockSpec(memory_space=pl.ANY)
    f32 = jnp.float32
    return pl.pallas_call(
        attend_kernel,
        out_shape=jax.ShapeDtypeStruct((blocks, BLK, heads * width), jnp.bfloat16),
        in_specs=[smem] * 3 + [vmem] * 3 + [hbm] * len(pieces),
        out_specs=vmem,
        scratch_shapes=[
            pltpu.VMEM((32, rows, width), jnp.bfloat16),
            pltpu.VMEM((32, rows, width), jnp.bfloat16),
            pltpu.VMEM((2, rows, 8 * BLK), f32),
            pltpu.VMEM((2, rows, 8 * BLK), f32),
            pltpu.VMEM((2, rows, 8 * BLK), jnp.bfloat16),
            pltpu.VMEM((2, rows, 8 * BLK), jnp.bfloat16),
            pltpu.VMEM((2, rows, 1), f32),
            pltpu.SemaphoreType.DMA((2, 8)),
        ],
        compiler_params=pltpu.CompilerParams(vmem_limit_bytes=24 * 2**20),
        cost_estimate=pl.CostEstimate(flops=2**31, bytes_accessed=24 * 2**20, transcendentals=2**21),
        name="attend",
    )(slots, vertical, diag, query, kpv, kpd, *pieces)


def ring(n, step):
    return [(i, (i + step) % n) for i in range(n)]


def after(arrays, dep):
    count = len(arrays)
    hbm = pl.BlockSpec(memory_space=pl.ANY)
    return pl.pallas_call(
        lambda *refs: None,
        out_shape=[jax.ShapeDtypeStruct(a.shape, a.dtype) for a in arrays],
        in_specs=[hbm] * (count + 1),
        out_specs=[hbm] * count,
        input_output_aliases={i: i for i in range(count)},
        name="after",
    )(*arrays, dep)


def up(a):
    return lax.ppermute(a, "tp", ring(lax.axis_size("tp"), 1))


def down(a):
    return lax.ppermute(a, "tp", ring(lax.axis_size("tp"), -1))


def project_kernel(steps, last, place_ref, *refs):
    rows, refs = refs[:8], refs[8:]
    count = len(steps)
    parts = 2 if last else 1
    weights, refs = refs[: count * parts], refs[count * parts :]
    if last:
        before, outs, (wbuf, sems) = refs[0], refs[1:9], refs[9:]
    else:
        acc, wbuf, sems = refs
    n, group, depth = rows[0].shape
    tp = place_ref[0]
    copies = [
        pltpu.make_async_copy(
            w, wbuf.at[i // parts, pl.ds((i % parts) * (depth // parts), depth // parts)], sems.at[i]
        )
        for i, w in enumerate(weights)
    ]
    for c in copies:
        c.start()
    def product(i, hops):
        k = lax.rem(tp + hops + n, n)
        a = jnp.concatenate([r[k] for r in rows], axis=0)
        return jnp.dot(a, wbuf[i], preferred_element_type=jnp.float32)

    if last:
        for c in copies:
            c.wait()
        total = before[...] + product(0, steps[0])
        for r, out in enumerate(outs):
            out[...] = total[r * group : (r + 1) * group].astype(jnp.bfloat16)
    else:
        copies[0].wait()
        acc[...] = product(0, 0)

        def add(i, carry):
            pltpu.make_async_copy(wbuf.at[i], wbuf.at[i], sems.at[i]).wait()
            hops = (i + 1) // 2
            acc[...] += product(i, jnp.where(i % 2 == 1, -hops, hops))
            return carry

        lax.fori_loop(1, count, add, 0)


def project(rows, weights, place, steps, before=None):
    n, group, depth = rows[0].shape
    last = before is not None
    cols = weights[0].shape[1]
    vmem = pl.BlockSpec(memory_space=pltpu.VMEM)
    hbm = pl.BlockSpec(memory_space=pltpu.HBM)
    if last:
        shapes = [jax.ShapeDtypeStruct((group, cols), jnp.bfloat16)] * 8
    else:
        shapes = jax.ShapeDtypeStruct((8 * group, cols), jnp.float32)
    return pl.pallas_call(
        functools.partial(project_kernel, steps, last),
        out_shape=shapes,
        in_specs=[pl.BlockSpec(memory_space=pltpu.SMEM)]
        + [vmem] * 8
        + [hbm] * len(weights)
        + [vmem] * last,
        out_specs=[vmem] * 8 if last else vmem,
        scratch_shapes=[
            pltpu.VMEM((len(steps), depth, cols), jnp.bfloat16),
            pltpu.SemaphoreType.DMA((len(weights),)),
        ],
        compiler_params=pltpu.CompilerParams(vmem_limit_bytes=32 * 2**20),
        cost_estimate=pl.CostEstimate(
            flops=2**29 * len(steps), bytes_accessed=2**21 * len(steps), transcendentals=0
        ),
        name="project",
    )(place, *rows, *weights, *([before] if last else []))


def per_device(query, keyval, vert_blocks, slash_offsets, counts, out_weight):
    heads, rows, width = query.shape
    seq_index = lax.axis_index("seq")
    tp_index = lax.axis_index("tp")
    core = seq_index % NC
    x_odd = (seq_index // NC) % 2
    y_odd = (seq_index // (NC * NX)) % 2
    block = y_odd * 2 + x_odd
    cols = out_weight.shape[1] // 8
    depth = out_weight.shape[0] // 2
    kv_head = tp_index // (lax.axis_size("tp") // keyval.shape[1])
    own = lax.dynamic_index_in_dim(keyval, kv_head, 1, keepdims=False)
    w0 = lax.dynamic_slice_in_dim(out_weight, (block * 2 + core) * cols, cols, 1)
    near = [own, send(own, A_UP), send(own, A_DOWN), send(own, A_FAR)]
    w_u1, w_d1 = up(w0), down(w0)
    line_k, line_v = (jnp.stack([a[i] for a in near]) for i in range(2))
    up_k, down_v = send(line_k, B_UP), send(line_v, B_DOWN)
    down_k, up_v = send(line_k, B_DOWN), send(line_v, B_UP)
    far_k, far_v = send(up_k, B_UP), send(down_v, B_DOWN)
    pieces = [line_k, up_k, down_k, far_k, line_v, up_v, down_v, far_v]
    pieces += [send(a, SWAP) for a in pieces]
    w_u1, w_d1 = after([w_u1, w_d1], up_k)
    w_u2, w_d2 = up(w_u1), down(w_d1)

    def mine(a):
        return lax.dynamic_slice_in_dim(a, tp_index * heads, heads, 0)

    attended = attend(
        query, pieces, shard_slots(seq_index), mine(vert_blocks), mine(slash_offsets),
        mine(counts), seq_index,
    )
    w_u2, w_d2 = after([w_u2, w_d2], attended)
    w_u3, w_d3 = up(w_u2), down(w_d2)
    tokens = lax.all_to_all(attended, "tp", split_axis=0, concat_axis=0, tiled=True)
    w_u4, w_d4 = up(w_u3[:depth]), down(w_d3[depth:])
    group = [tokens] + [send(tokens, partner(r, 0)) for r in (1, 2, 3)]
    group += [send(a, SWAP) for a in group]
    place = jnp.stack([tp_index, core])
    early = [w0, w_u1, w_d1, w_u2, w_d2, w_u3, w_d3]
    total = project(group, early, place, (0, -1, 1, -2, 2, -3, 3))
    out = project(group, [w_u4, w_d4], place, (4,), total)
    ours = [out[0]] + [send(out[r], partner(r, 0)) for r in (1, 2, 3)]
    theirs = [send(out[r + 4], partner(r, 1)) for r in range(4)]
    first, odd_x, odd_y = core == 0, x_odd == 1, y_odd == 1
    wide = [
        jnp.concatenate([jnp.where(first, a, b), jnp.where(first, b, a)], axis=1)
        for a, b in zip(ours, theirs)
    ]
    wide = [jnp.where(odd_x, wide[i ^ 1], wide[i]) for i in range(4)]
    return jnp.concatenate([jnp.where(odd_y, wide[i ^ 2], wide[i]) for i in range(4)], axis=1)


def solution(mesh):
    return jax.shard_map(
        per_device,
        mesh=mesh,
        in_specs=(P("tp", "seq", None), P(None, None, "seq", None), P(), P(), P(), P("tp", None)),
        out_specs=P(("seq", "tp"), None),
        check_vma=False,
    )
```

```python
import functools
import math

import jax
import jax.numpy as jnp
from jax import lax
from jax.experimental import pallas as pl
from jax.experimental.pallas import tpu as pltpu
from jax.sharding import PartitionSpec as P

BLK = 64
NY, NX, NC = 4, 4, 2
DEAD = 1 << 20
SCALE = math.log2(math.e)


def seq_perm(move):
    pairs = []
    for y in range(NY):
        for x in range(NX):
            for c in range(NC):
                ty, tx, tc = move(y, x, c)
                pairs.append(((y * NX + x) * NC + c, ((ty % NY) * NX + tx % NX) * NC + tc))
    return pairs


A_UP = seq_perm(lambda y, x, c: (y, x + 1, c) if c == 0 else (y + 1, x, c))
A_DOWN = seq_perm(lambda y, x, c: (y, x - 1, c) if c == 0 else (y - 1, x, c))
A_FAR = seq_perm(lambda y, x, c: (y, x + 2, c) if c == 0 else (y + 2, x, c))
B_UP = seq_perm(lambda y, x, c: (y + 1, x, c) if c == 0 else (y, x + 1, c))
B_DOWN = seq_perm(lambda y, x, c: (y - 1, x, c) if c == 0 else (y, x - 1, c))
def pair(v, c):
    return (v ^ 1) if c == 0 else (v + 1 if v % 2 else v - 1)


def partner(r, other):
    return seq_perm(
        lambda y, x, c: (
            pair(y, c ^ other) if r & 2 else y,
            pair(x, c ^ other) if r & 1 else x,
            c ^ other,
        )
    )


SWAP = seq_perm(lambda y, x, c: (y, x, 1 - c))


def send(a, pairs):
    return lax.ppermute(a, "seq", pairs)


def shard_slots(seq_index):
    shard = jnp.arange(NY * NX * NC, dtype=jnp.int32)

    def parts(i):
        return i // (NX * NC), (i // NC) % NX, i % NC

    ys, xs, cs = parts(shard)
    y0, x0, c0 = parts(seq_index)
    order = jnp.array([0, 2, 3, 1], jnp.int32)
    in_y, in_x = order[(ys - y0) % NY], order[(xs - x0) % NX]
    first = jnp.where(cs == 0, in_x, in_y)
    second = jnp.where(cs == 0, in_y, in_x)
    return (cs != c0) * 16 + second * 4 + first


def attend_kernel(slots_ref, vert_ref, diag_ref, q_ref, kpv_ref, kpd_ref, *refs):
    pieces, o_ref = refs[:16], refs[16]
    kbuf, vbuf, sv_ref, sd_ref, pv_ref, pd_ref, tot_ref, sems = refs[17:]
    heads, rows, width = q_ref.shape
    blocks = rows // BLK
    per = rows // BLK
    copies = ([], [])
    for side in range(2):
        for which, buf in enumerate((kbuf, vbuf)):
            for j in range(4):
                src = pieces[side * 8 + which * 4 + j]
                copies[which].append(
                    pltpu.make_async_copy(
                        src, buf.at[pl.ds(side * 16 + j * 4, 4)], sems.at[which, side * 4 + j]
                    )
                )
    for c in copies[0] + copies[1]:
        c.start()
    for c in copies[0]:
        c.wait()

    def tile(buf, block):
        return buf[slots_ref[block // per], pl.ds(pl.multiple_of((block % per) * BLK, BLK), BLK), :]

    scale = SCALE / math.sqrt(width)
    nt = (((1,), (1,)), ((), ()))

    def one_head(h, carry):
        verts = [vert_ref[h, c] for c in range(8)]
        diags = [[diag_ref[h * blocks + b, c] for c in range(8)] for b in range(blocks)]
        sv, sd, pv, pd, tot = (r.at[h % 2] for r in (sv_ref, sd_ref, pv_ref, pd_ref, tot_ref))
        k_v = jnp.concatenate([tile(kbuf, v) for v in verts], axis=0)
        sv[...] = lax.dot_general(q_ref[h], k_v, nt, preferred_element_type=jnp.float32)
        for b in range(blocks):
            r = slice(b * BLK, (b + 1) * BLK)
            k_d = jnp.concatenate([tile(kbuf, v) for v in diags[b]], axis=0)
            sd[r, :] = lax.dot_general(q_ref[h, r, :], k_d, nt, preferred_element_type=jnp.float32)
        kpv = kpv_ref[h]
        for b in range(blocks):
            r = slice(b * BLK, (b + 1) * BLK)
            qpos = b * BLK + lax.broadcasted_iota(jnp.int32, (BLK, 1), 0)
            s_d = jnp.where(kpd_ref[h * blocks + b] <= qpos, sd[r, :], -1e30)
            s_v = jnp.where(kpv <= qpos, sv[r, :], -1e30)
            top = jnp.maximum(
                jnp.max(s_d, axis=1, keepdims=True), jnp.max(s_v, axis=1, keepdims=True)
            )
            p_d = jnp.exp2((s_d - top) * scale)
            p_v = jnp.exp2((s_v - top) * scale)
            tot[r, :] = jnp.sum(p_d, axis=1, keepdims=True) + jnp.sum(p_v, axis=1, keepdims=True)
            pv[r, :] = p_v.astype(jnp.bfloat16)
            pd[r, :] = p_d.astype(jnp.bfloat16)

        @pl.when(h == 0)
        def _():
            for c in copies[1]:
                c.wait()

        v_v = jnp.concatenate([tile(vbuf, v) for v in verts], axis=0)
        o_v = jnp.dot(pv[...], v_v, preferred_element_type=jnp.float32)
        for b in range(blocks):
            r = slice(b * BLK, (b + 1) * BLK)
            v_d = jnp.concatenate([tile(vbuf, v) for v in diags[b]], axis=0)
            o_d = jnp.dot(pd[r, :], v_d, preferred_element_type=jnp.float32)
            o = ((o_v[r] + o_d) / tot[r, :]).astype(jnp.bfloat16)
            o_ref[b, :, pl.ds(pl.multiple_of(h * width, width), width)] = o
        return carry

    lax.fori_loop(0, heads, one_head, 0)


def attend(query, pieces, slots, vertical, slash, counts, seq_index):
    heads, rows, width = query.shape
    blocks = rows // BLK
    slot = jnp.arange(8, dtype=jnp.int32)
    first = seq_index * blocks
    vert_live = slot[None, :] < counts[:, 0:1]
    diag = first + jnp.arange(blocks, dtype=jnp.int32)[None, :, None] - slash[:, None, :]
    covered = jnp.any(
        (diag[:, :, :, None] == vertical[:, None, None, :]) & vert_live[:, None, None, :], axis=3
    )
    diag_live = (slot < counts[:, 1:2])[:, None, :] & (diag >= 0) & jnp.logical_not(covered)
    within = jnp.arange(BLK, dtype=jnp.int32)
    kpv = jnp.where(
        vert_live[:, :, None], (vertical - first)[:, :, None] * BLK + within, DEAD
    ).reshape(heads, 1, 8 * BLK)
    kpd = jnp.where(
        diag_live[:, :, :, None], (diag - first)[:, :, :, None] * BLK + within, DEAD
    ).reshape(heads * blocks, 1, 8 * BLK)
    diag = jnp.maximum(diag, 0).reshape(heads * blocks, 8)
    smem = pl.BlockSpec(memory_space=pltpu.SMEM)
    vmem = pl.BlockSpec(memory_space=pltpu.VMEM)
    hbm = pl.BlockSpec(memory_space=pl.ANY)
    f32 = jnp.float32
    return pl.pallas_call(
        attend_kernel,
        out_shape=jax.ShapeDtypeStruct((blocks, BLK, heads * width), jnp.bfloat16),
        in_specs=[smem] * 3 + [vmem] * 3 + [hbm] * len(pieces),
        out_specs=vmem,
        scratch_shapes=[
            pltpu.VMEM((32, rows, width), jnp.bfloat16),
            pltpu.VMEM((32, rows, width), jnp.bfloat16),
            pltpu.VMEM((2, rows, 8 * BLK), f32),
            pltpu.VMEM((2, rows, 8 * BLK), f32),
            pltpu.VMEM((2, rows, 8 * BLK), jnp.bfloat16),
            pltpu.VMEM((2, rows, 8 * BLK), jnp.bfloat16),
            pltpu.VMEM((2, rows, 1), f32),
            pltpu.SemaphoreType.DMA((2, 8)),
        ],
        compiler_params=pltpu.CompilerParams(vmem_limit_bytes=24 * 2**20),
        cost_estimate=pl.CostEstimate(flops=2**31, bytes_accessed=24 * 2**20, transcendentals=2**21),
        name="attend",
    )(slots, vertical, diag, query, kpv, kpd, *pieces)


def ring(n, step):
    return [(i, (i + step) % n) for i in range(n)]


def after(arrays, dep):
    count = len(arrays)
    hbm = pl.BlockSpec(memory_space=pl.ANY)
    return pl.pallas_call(
        lambda *refs: None,
        out_shape=[jax.ShapeDtypeStruct(a.shape, a.dtype) for a in arrays],
        in_specs=[hbm] * (count + 1),
        out_specs=[hbm] * count,
        input_output_aliases={i: i for i in range(count)},
        name="after",
    )(*arrays, dep)


def up(a):
    return lax.ppermute(a, "tp", ring(lax.axis_size("tp"), 1))


def down(a):
    return lax.ppermute(a, "tp", ring(lax.axis_size("tp"), -1))


def project_kernel(steps, last, place_ref, *refs):
    rows, refs = refs[:8], refs[8:]
    count = len(steps)
    parts = 2 if last else 1
    weights, refs = refs[: count * parts], refs[count * parts :]
    if last:
        before, outs, (wbuf, sems) = refs[0], refs[1:9], refs[9:]
    else:
        acc, wbuf, sems = refs
    n, group, depth = rows[0].shape
    tp = place_ref[0]
    copies = [
        pltpu.make_async_copy(
            w, wbuf.at[i // parts, pl.ds((i % parts) * (depth // parts), depth // parts)], sems.at[i]
        )
        for i, w in enumerate(weights)
    ]
    for c in copies:
        c.start()
    def product(i, hops):
        k = lax.rem(tp + hops + n, n)
        a = jnp.concatenate([r[k] for r in rows], axis=0)
        return jnp.dot(a, wbuf[i], preferred_element_type=jnp.float32)

    if last:
        for c in copies:
            c.wait()
        total = before[...] + product(0, steps[0])
        for r, out in enumerate(outs):
            out[...] = total[r * group : (r + 1) * group].astype(jnp.bfloat16)
    else:
        copies[0].wait()
        acc[...] = product(0, 0)

        def add(i, carry):
            pltpu.make_async_copy(wbuf.at[i], wbuf.at[i], sems.at[i]).wait()
            hops = (i + 1) // 2
            acc[...] += product(i, jnp.where(i % 2 == 1, -hops, hops))
            return carry

        lax.fori_loop(1, count, add, 0)


def project(rows, weights, place, steps, before=None):
    n, group, depth = rows[0].shape
    last = before is not None
    cols = weights[0].shape[1]
    vmem = pl.BlockSpec(memory_space=pltpu.VMEM)
    hbm = pl.BlockSpec(memory_space=pltpu.HBM)
    if last:
        shapes = [jax.ShapeDtypeStruct((group, cols), jnp.bfloat16)] * 8
    else:
        shapes = jax.ShapeDtypeStruct((8 * group, cols), jnp.float32)
    return pl.pallas_call(
        functools.partial(project_kernel, steps, last),
        out_shape=shapes,
        in_specs=[pl.BlockSpec(memory_space=pltpu.SMEM)]
        + [vmem] * 8
        + [hbm] * len(weights)
        + [vmem] * last,
        out_specs=[vmem] * 8 if last else vmem,
        scratch_shapes=[
            pltpu.VMEM((len(steps), depth, cols), jnp.bfloat16),
            pltpu.SemaphoreType.DMA((len(weights),)),
        ],
        compiler_params=pltpu.CompilerParams(vmem_limit_bytes=32 * 2**20),
        cost_estimate=pl.CostEstimate(
            flops=2**29 * len(steps), bytes_accessed=2**21 * len(steps), transcendentals=0
        ),
        name="project",
    )(place, *rows, *weights, *([before] if last else []))


def per_device(query, keyval, vert_blocks, slash_offsets, counts, out_weight):
    heads, rows, width = query.shape
    seq_index = lax.axis_index("seq")
    tp_index = lax.axis_index("tp")
    core = seq_index % NC
    x_odd = (seq_index // NC) % 2
    y_odd = (seq_index // (NC * NX)) % 2
    block = y_odd * 2 + x_odd
    cols = out_weight.shape[1] // 8
    depth = out_weight.shape[0] // 2
    kv_head = tp_index // (lax.axis_size("tp") // keyval.shape[1])
    own = lax.dynamic_index_in_dim(keyval, kv_head, 1, keepdims=False)
    w0 = lax.dynamic_slice_in_dim(out_weight, (block * 2 + core) * cols, cols, 1)
    near = [own, send(own, A_UP), send(own, A_DOWN), send(own, A_FAR)]
    w_u1, w_d1 = up(w0), down(w0)
    line_k, line_v = (jnp.stack([a[i] for a in near]) for i in range(2))
    up_k, down_v = send(line_k, B_UP), send(line_v, B_DOWN)
    down_k, up_v = send(line_k, B_DOWN), send(line_v, B_UP)
    far_k, far_v = send(up_k, B_UP), send(down_v, B_DOWN)
    pieces = [line_k, up_k, down_k, far_k, line_v, up_v, down_v, far_v]
    pieces += [send(a, SWAP) for a in pieces]
    w_u2, w_d2 = up(w_u1), down(w_d1)

    def mine(a):
        return lax.dynamic_slice_in_dim(a, tp_index * heads, heads, 0)

    attended = attend(
        query, pieces, shard_slots(seq_index), mine(vert_blocks), mine(slash_offsets),
        mine(counts), seq_index,
    )
    w_u2, w_d2 = after([w_u2, w_d2], attended)
    w_u3, w_d3 = up(w_u2), down(w_d2)
    tokens = lax.all_to_all(attended, "tp", split_axis=0, concat_axis=0, tiled=True)
    w_u4, w_d4 = up(w_u3[:depth]), down(w_d3[depth:])
    group = [tokens] + [send(tokens, partner(r, 0)) for r in (1, 2, 3)]
    group += [send(a, SWAP) for a in group]
    place = jnp.stack([tp_index, core])
    early = [w0, w_u1, w_d1, w_u2, w_d2, w_u3, w_d3]
    total = project(group, early, place, (0, -1, 1, -2, 2, -3, 3))
    out = project(group, [w_u4, w_d4], place, (4,), total)
    ours = [out[0]] + [send(out[r], partner(r, 0)) for r in (1, 2, 3)]
    theirs = [send(out[r + 4], partner(r, 1)) for r in range(4)]
    first, odd_x, odd_y = core == 0, x_odd == 1, y_odd == 1
    wide = [
        jnp.concatenate([jnp.where(first, a, b), jnp.where(first, b, a)], axis=1)
        for a, b in zip(ours, theirs)
    ]
    wide = [jnp.where(odd_x, wide[i ^ 1], wide[i]) for i in range(4)]
    return jnp.concatenate([jnp.where(odd_y, wide[i ^ 2], wide[i]) for i in range(4)], axis=1)


def solution(mesh):
    return jax.shard_map(
        per_device,
        mesh=mesh,
        in_specs=(P("tp", "seq", None), P(None, None, "seq", None), P(), P(), P(), P("tp", None)),
        out_specs=P(("seq", "tp"), None),
        check_vma=False,
    )
```
